256 devices in a mesh: grp: 8 (over x, core), tile: 32 (over z, y).
Axes of the slice: x: 4, y: 4, z: 8, core: 2. Of those that a mesh axis runs over, the one named last changes fastest.
Arguments:
- features: bfloat16 [65536, 1024], P(('grp', 'tile'))
- projection: bfloat16 [1024, 768], replicated, may hold values from -0.1875 to 0.1875
- pooled_grad: bfloat16 [96, 768, 768], P('grp', 'tile'), may hold values from -96 to 96
- slide_counts: int32 [96], P('grp'), may hold values from 321 to 2176, as said below
- slide_offsets: int32 [96], P('grp'), may hold values from 0 to 7808, as said below
Outputs:
- feature_grad: bfloat16 [65536, 1024], P(('grp', 'tile'))
- projection_grad: float32 [1024, 768], replicated
The draws below stay inside these ranges and needn't reach their ends.
Inputs may be any that keep to these rules, and one draw needn't show every extreme that they name: Within each group the slides lie end to end from row 0 and fill all 8192 rows in order; each slide spans a multiple of 128 rows, at least 384, and the last slide of each group exactly 384; slide_offsets gives each slide's first row within its group. A slide's first slide_counts rows are tiles, the rest of its span, fewer than 64 rows, is padding; a largest slide of each group, never the last, has no padding.
All inputs are finite; a program needn't handle non-finite values.
Results may differ from the reference program's by a relative error of at most 0.011.
Values may be sent and summed in bfloat16 or wider, within the bound.
No kernel may reach another device: no remote copies, remote signals or barrier semaphores. Data moves between devices by JAX's collectives and lax.ppermute only.
A program may use at most 256 MiB of HBM per device.

```python
import jax
import jax.numpy as jnp
from jax import lax

DIN = 1024
D = 768
BLOCK = 128
ROWS = 256
SLIDES = 12
SLIDES_ALL = 96
GROUP_ROWS = 8192
TILES = 65536


def slide_layout(key):
    groups = SLIDES_ALL // SLIDES
    least = ROWS // BLOCK + 1
    extra = GROUP_ROWS // BLOCK - SLIDES * least
    lead_extra = (extra + 1) // 2
    rest_extra = extra - lead_extra
    pick_key = jax.random.fold_in(key, 101)
    pad_key = jax.random.fold_in(key, 202)
    lead_key = jax.random.fold_in(key, 303)
    lead_pos = jax.random.randint(lead_key, (groups, 1), 0, SLIDES - 1)
    picks = jax.random.randint(pick_key, (groups, rest_extra), 0, SLIDES - 2)
    picks = picks + (picks >= lead_pos).astype(jnp.int32)
    slide_ids = jnp.arange(SLIDES, dtype=jnp.int32)
    picked = jnp.sum((picks[:, :, None] == slide_ids[None, None, :]).astype(jnp.int32), axis=1)
    is_lead = slide_ids[None, :] == lead_pos
    lead = jnp.where(is_lead, lead_extra, 0).astype(jnp.int32)
    blocks = least + picked + lead
    spans = blocks * BLOCK
    padding = jax.random.randint(pad_key, (groups, SLIDES), 0, BLOCK // 2)
    padding = jnp.where(is_lead, 0, padding)
    padding = jnp.where(slide_ids[None, :] == SLIDES - 1, BLOCK // 2 - 1, padding)
    counts = spans - padding
    offsets = jnp.cumsum(spans, axis=1) - spans
    return (counts.reshape(-1).astype(jnp.int32), offsets.reshape(-1).astype(jnp.int32))


def draw_slide_counts(key, part):
    counts, offsets = slide_layout(key)
    return counts


def draw_slide_offsets(key, part):
    counts, offsets = slide_layout(key)
    return offsets


def draw_features(key, part):
    key = jax.random.fold_in(key, 7)
    base_key, dir_key, coef_key, scale_key = jax.random.split(key, 4)
    base = jax.random.normal(base_key, (TILES, DIN), jnp.float32)
    strength = 6.0
    low, high = (0.5, 5.0)
    direction = jax.random.normal(dir_key, (DIN,), jnp.float32) * DIN ** (-0.5)
    coef = jax.random.normal(coef_key, (TILES, 1), jnp.float32)
    row_scale = jnp.exp(jax.random.uniform(scale_key, (TILES, 1), jnp.float32, jnp.log(low), jnp.log(high)))
    values = (base + strength * coef * direction[None, :]) * row_scale
    return values.astype(jnp.bfloat16)


def block_scale(rng, dims, shards, low, largest):
    def one(dim, parts):
        heights = jax.random.uniform(jax.random.fold_in(jax.random.fold_in(rng, 6), dim), (parts,), jnp.float32, low / len(shards), largest / len(shards))
        return jnp.repeat(jnp.exp(heights), dims[dim] // parts).reshape((-1,) + (1,) * (len(dims) - dim - 1))

    factor_of = one(*shards[0])
    for cut in shards[1:]:
        factor_of = factor_of * one(*cut)
    return factor_of


def bell_draw(rng, dims, spread, most, cuts=(), kind=jnp.bfloat16):
    loudness = block_scale(rng, dims, cuts, -0.22, 0.18) if cuts else 1.0
    entries = jax.random.normal(rng, dims, jnp.float32) * spread * loudness
    return jnp.minimum(jnp.maximum(entries, -most), most).astype(kind)


def setup_inputs(seed: int = 0) -> dict:
    key_list = jax.random.split(jax.random.key(seed), 6)
    return {
        "features": draw_features(jax.random.fold_in(key_list[5], 71), 0),
        "projection": bell_draw(key_list[1], (DIN, D), DIN ** -0.5, 0.1875),
        "pooled_grad": bell_draw(key_list[2], (SLIDES_ALL, D, D), 16.0, 96.0, ((0, 8), (1, 32))),
        "slide_counts": draw_slide_counts(jax.random.fold_in(key_list[5], 71), 0),
        "slide_offsets": draw_slide_offsets(jax.random.fold_in(key_list[5], 71), 0),
    }


def pool_backward(sq_sum, row_sum, count, grads):
    mean_vec = row_sum / count
    covar = sq_sum / count - mean_vec[:, None] * mean_vec[None, :]
    norm_value = jnp.sqrt(jnp.sum(covar * covar) + 1e-06)
    scaled = covar / norm_value
    scaled_b = scaled.astype(grads.dtype)
    first_iter = 1.5 * scaled - 0.5 * jnp.dot(scaled_b, scaled_b, preferred_element_type=jnp.float32)
    first_b = first_iter.astype(grads.dtype)
    second_iter = 1.5 * first_iter - 0.5 * jnp.dot(scaled_b, first_b, preferred_element_type=jnp.float32)
    second_b = second_iter.astype(grads.dtype)
    grad_top = jnp.sqrt(norm_value) * grads.astype(jnp.float32)
    grad_top_b = grad_top.astype(grads.dtype)
    right_term = jnp.dot(grad_top_b, second_b.T, preferred_element_type=jnp.float32)
    grad_second = -0.5 * jnp.dot(first_b.T, grad_top_b, preferred_element_type=jnp.float32)
    grad_second_b = grad_second.astype(grads.dtype)
    grad_first = 1.5 * grad_top - 0.5 * right_term + 1.5 * grad_second - 0.5 * jnp.dot(scaled_b.T, grad_second_b, preferred_element_type=jnp.float32)
    grad_first_b = grad_first.astype(grads.dtype)
    grad_scaled = -0.5 * jnp.dot(grad_second_b, first_b.T, preferred_element_type=jnp.float32) + 1.5 * grad_first
    grad_scaled = grad_scaled - 0.5 * (jnp.dot(grad_first_b, scaled_b.T, preferred_element_type=jnp.float32) + jnp.dot(scaled_b.T, grad_first_b, preferred_element_type=jnp.float32))
    grad_norm = (1.5 * jnp.sum(grad_top * first_iter) - 0.5 * jnp.sum(right_term * first_b.astype(jnp.float32))) / (2.0 * norm_value)
    grad_norm = grad_norm - jnp.sum(grad_scaled * scaled) / norm_value
    grad_covar = (grad_scaled + grad_norm * covar) / norm_value
    sym_grad = (grad_covar + grad_covar.T) / count
    mean_grad = -jnp.dot(sym_grad, mean_vec, precision=lax.Precision.HIGHEST)
    return (sym_grad.astype(grads.dtype), mean_grad)

def reference(features, projection, pooled_grad, slide_counts, slide_offsets):
    groups = SLIDES_ALL // SLIDES
    block_count = GROUP_ROWS // BLOCK
    mixed = jnp.dot(features, projection, preferred_element_type=jnp.float32).astype(features.dtype)

    def per_group(pieces):
        rows_x, counts, offsets, grads = pieces
        positions = jnp.arange(GROUP_ROWS, dtype=jnp.int32)
        row_slide = (lax.optimization_barrier(jnp.sum((offsets[None, :] <= positions[:, None]).astype(jnp.int32), axis=1)) - 1).astype(jnp.int32)
        valid = positions - offsets[row_slide] < counts[row_slide]
        masked = jnp.where(valid[:, None], rows_x, jnp.zeros((), rows_x.dtype))
        blocks = masked.reshape(block_count, BLOCK, D).astype(jnp.float32)
        block_slide = row_slide.reshape(block_count, BLOCK)[:, 0]
        one_hot = (block_slide[None, :] == jnp.arange(SLIDES, dtype=jnp.int32)[:, None]).astype(jnp.float32)
        block_sq = jnp.einsum('brd,bre->bde', blocks, blocks, precision=lax.Precision.HIGHEST)
        sq_sum = jnp.einsum('sb,bde->sde', one_hot, block_sq, precision=lax.Precision.HIGHEST)
        row_sum = jnp.einsum('sb,bd->sd', one_hot, lax.optimization_barrier(jnp.sum(blocks, axis=1)), precision=lax.Precision.HIGHEST)
        sym_b, mean_grad = lax.map(lambda args: pool_backward(*args), (sq_sum, row_sum, counts.astype(jnp.float32), grads))
        block_q = sym_b[block_slide].astype(jnp.float32)
        result = jnp.einsum('brd,bde->bre', blocks, block_q, precision=lax.Precision.HIGHEST).reshape(GROUP_ROWS, D)
        result = result + mean_grad[row_slide]
        return jnp.where(valid[:, None], result, 0.0).astype(rows_x.dtype)
    row_grad = lax.map(per_group, (mixed.reshape(groups, GROUP_ROWS, D), slide_counts.reshape(groups, SLIDES), slide_offsets.reshape(groups, SLIDES), pooled_grad.reshape(groups, SLIDES, D, D)))
    row_grad = row_grad.reshape(TILES, D)
    feature_grad = jnp.dot(row_grad, projection.T, preferred_element_type=jnp.float32).astype(features.dtype)
    projection_grad = jnp.dot(features.T, row_grad, preferred_element_type=jnp.float32)
    return (feature_grad, projection_grad)
```

```python
import jax
import jax.numpy as jnp
from jax import lax
from jax.sharding import PartitionSpec as P

BLOCK = 128


def entering(value, axis, join, neutral):
    count = lax.axis_size(axis)
    place = lax.axis_index(axis)
    ahead = count - 1 - place
    gathered = jax.tree.map(
        lambda a, kind: lax.all_gather(a.astype(kind), axis),
        value,
        (jnp.bfloat16, jnp.bfloat16, jnp.bfloat16),
    )
    state = jax.tree.map(lambda a, e: jnp.zeros_like(a) + jnp.asarray(e, a.dtype), value, neutral)

    def entering_one(lap, state):
        source = count - 1 - lap
        return join(
            state,
            jax.tree.map(
                lambda a, own: lax.dynamic_index_in_dim(a, source, 0, False).astype(own.dtype),
                gathered,
                value,
            ),
        )

    return lax.fori_loop(0, ahead, entering_one, state)


def prefix(value, axis, join, neutral):
    place = lax.axis_index(axis)
    gathered = jax.tree.map(
        lambda a, kind: lax.all_gather(a.astype(kind), axis),
        value,
        jax.tree.map(lambda a: jnp.bfloat16 if a.dtype == jnp.float32 else a.dtype, value),
    )
    state = jax.tree.map(lambda a, e: jnp.zeros_like(a) + jnp.asarray(e, a.dtype), value, neutral)

    def prefix_one(lap, state):
        return join(
            state,
            jax.tree.map(
                lambda a, own: lax.dynamic_index_in_dim(a, lap, 0, False).astype(own.dtype),
                gathered,
                value,
            ),
        )

    return lax.fori_loop(0, place, prefix_one, state)


def pool_backward(sq_sum, row_sum, count, grads):
    mean_vec = row_sum / count
    covar = sq_sum / count - mean_vec[:, None] * mean_vec[None, :]
    norm_value = jnp.sqrt(jnp.sum(covar * covar) + 1e-06)
    scaled = covar / norm_value
    scaled_b = scaled.astype(jnp.bfloat16)
    first_iter = 1.5 * scaled - 0.5 * jnp.dot(
        scaled_b, scaled_b, preferred_element_type=jnp.float32
    )
    first_b = first_iter.astype(jnp.bfloat16)
    second_iter = 1.5 * first_iter - 0.5 * jnp.dot(
        scaled_b, first_b, preferred_element_type=jnp.float32
    )
    second_b = second_iter.astype(jnp.bfloat16)
    grad_top = jnp.sqrt(norm_value) * grads.astype(jnp.float32)
    grad_top_b = grad_top.astype(jnp.bfloat16)
    right_term = jnp.dot(grad_top_b, second_b.T, preferred_element_type=jnp.float32)
    grad_second = -0.5 * jnp.dot(first_b.T, grad_top_b, preferred_element_type=jnp.float32)
    grad_second_b = grad_second.astype(jnp.bfloat16)
    grad_first = (
        1.5 * grad_top
        - 0.5 * right_term
        + 1.5 * grad_second
        - 0.5 * jnp.dot(scaled_b.T, grad_second_b, preferred_element_type=jnp.float32)
    )
    grad_first_b = grad_first.astype(jnp.bfloat16)
    grad_scaled = (
        -0.5 * jnp.dot(grad_second_b, first_b.T, preferred_element_type=jnp.float32)
        + 1.5 * grad_first
    )
    grad_scaled = grad_scaled - 0.5 * (
        jnp.dot(grad_first_b, scaled_b.T, preferred_element_type=jnp.float32)
        + jnp.dot(scaled_b.T, grad_first_b, preferred_element_type=jnp.float32)
    )
    grad_norm = (
        1.5 * jnp.sum(grad_top * first_iter)
        - 0.5 * jnp.sum(right_term * first_b.astype(jnp.float32))
    ) / (2.0 * norm_value)
    grad_norm = grad_norm - jnp.sum(grad_scaled * scaled) / norm_value
    grad_covar = (grad_scaled + grad_norm * covar) / norm_value
    sym_grad = (grad_covar + grad_covar.T) / count
    mean_grad = -jnp.dot(sym_grad, mean_vec, precision=lax.Precision.HIGHEST)
    return (sym_grad.astype(jnp.bfloat16), mean_grad)


def pack_sym(full):
    half = full.shape[0] // 2
    upper = full[:half, :half]
    cross = full[half:, :half]
    lower = full[half:, half:]
    row_ids = jnp.arange(half, dtype=jnp.int32)[:, None]
    col_ids = jnp.arange(half, dtype=jnp.int32)[None, :]
    folded = jnp.where(row_ids >= col_ids, upper, lower.T)
    return jnp.concatenate([cross, folded, jnp.diagonal(lower)[None, :]], axis=0)


def unpack_sym(packed):
    half = packed.shape[1]
    cross = packed[:half]
    folded = packed[half : 2 * half]
    lower_diag = packed[2 * half]
    row_ids = jnp.arange(half, dtype=jnp.int32)[:, None]
    col_ids = jnp.arange(half, dtype=jnp.int32)[None, :]
    upper = jnp.where(row_ids >= col_ids, folded, folded.T)
    lower = jnp.where(
        row_ids > col_ids, folded.T, jnp.where(row_ids < col_ids, folded, lower_diag[None, :])
    )
    top = jnp.concatenate([upper, cross.T], axis=1)
    bottom = jnp.concatenate([cross, lower], axis=1)
    return jnp.concatenate([top, bottom], axis=0)


def add_chain(earlier, later):
    return (
        later[0] + later[2] * earlier[0],
        later[1] + later[2] * earlier[1],
        earlier[2] * later[2],
    )


def keep_nearest(earlier, later):
    passing = later[2] > 0.5
    return (
        jnp.where(passing, earlier[0], later[0]),
        jnp.where(passing, earlier[1], later[1]),
        earlier[2] * later[2],
    )

CORE_PAIRS = [(i, i ^ 1) for i in range(8)]


def x_shift(step):
    return [(x * 2 + c, (x + step) % 4 * 2 + c) for x in range(4) for c in range(2)]


def y_shift(step):
    return [(z * 4 + y, z * 4 + (y + step) % 4) for z in range(8) for y in range(4)]


Z_GROUPS = [[z * 4 + y for z in range(8)] for y in range(4)]


def scatter_four(value, axis, shift, place):
    rows = value.shape[0] // 4
    parts = value.reshape(4, rows, value.shape[1])
    sent = parts.astype(jnp.bfloat16)
    got = [
        lax.ppermute(lax.dynamic_index_in_dim(sent, (place + step) % 4, 0, False), axis, shift(step))
        for step in (1, 3, 2)
    ]
    total = lax.dynamic_index_in_dim(parts, place, 0, False)
    for one in got:
        total = total + one.astype(jnp.float32)
    return total


def gather_four(value, axis, shift, place):
    out = jnp.zeros((4,) + value.shape, value.dtype)
    got = [(step, lax.ppermute(value, axis, shift(step))) for step in (1, 3, 2)]
    out = lax.dynamic_update_index_in_dim(out, value, place, 0)
    for step, one in got:
        out = lax.dynamic_update_index_in_dim(out, one, (place - step) % 4, 0)
    return out.reshape(4 * value.shape[0], value.shape[1])


def reduce_everywhere(term):
    group = lax.axis_index("grp")
    core = group % 2
    x_place = group // 2
    y_place = lax.axis_index("tile") % 4
    halves = term.reshape(2, term.shape[0] // 2, term.shape[1])
    other = lax.dynamic_index_in_dim(halves, 1 - core, 0, False).astype(jnp.bfloat16)
    mine = lax.dynamic_index_in_dim(halves, core, 0, False)
    total = mine + lax.ppermute(other, "grp", CORE_PAIRS).astype(jnp.float32)
    total = scatter_four(total, "grp", x_shift, x_place)
    total = scatter_four(total, "tile", y_shift, y_place)
    sent = jnp.broadcast_to(total.astype(jnp.bfloat16)[None], (8,) + total.shape)
    got = lax.all_to_all(sent, "tile", 0, 0, axis_index_groups=Z_GROUPS, tiled=True)
    value = jnp.sum(got.astype(jnp.float32), axis=0).astype(jnp.bfloat16)
    value = gather_four(value, "tile", y_shift, y_place)
    value = gather_four(value, "grp", x_shift, x_place)
    theirs = lax.ppermute(value, "grp", CORE_PAIRS)
    low = jnp.where(core == 0, value, theirs)
    high = jnp.where(core == 0, theirs, value)
    return jnp.concatenate([low, high], axis=0).astype(jnp.float32)


def shards(features, projection, pooled_grad, slide_counts, slide_offsets):
    tile_count = lax.axis_size("tile")
    rows = features.shape[0]
    width = projection.shape[1]
    block_count = rows // BLOCK
    slide_total = slide_offsets.shape[0]
    group_rows = rows * tile_count
    first_row = lax.axis_index("tile") * rows
    slide_ends = jnp.concatenate([slide_offsets[1:], jnp.full((1,), group_rows, jnp.int32)])

    def slide_of(places):
        return jnp.sum((slide_offsets[None, :] <= places[:, None]).astype(jnp.int32), axis=1) - 1

    positions = first_row + jnp.arange(rows, dtype=jnp.int32)
    row_slide = slide_of(positions)
    one_hot = (row_slide[:, None] == jnp.arange(slide_total, dtype=jnp.int32)[None, :]).astype(
        jnp.int32
    )
    row_start = jnp.sum(one_hot * slide_offsets[None, :], axis=1)
    row_limit = jnp.sum(one_hot * slide_counts[None, :], axis=1)
    valid = positions - row_start < row_limit
    edge_slides = slide_of(jnp.stack([first_row, first_row + rows - 1]))
    slot_first = edge_slides[0]
    slot_last = edge_slides[1]
    same_slide = slot_first == slot_last
    from_left = slide_offsets[slot_first] < first_row
    to_right = slide_ends[slot_last] > first_row + rows
    owns = slide_offsets[slot_last] >= first_row
    passing = (same_slide & from_left & to_right).astype(jnp.float32)
    count_real = slide_counts.astype(jnp.float32)
    mixed = jnp.dot(features, projection, preferred_element_type=jnp.float32).astype(jnp.bfloat16)
    masked = jnp.where(valid[:, None], mixed, jnp.zeros((), jnp.bfloat16))
    blocks = masked.reshape(block_count, BLOCK, width)
    block_second = row_slide.reshape(block_count, BLOCK)[:, 0] != slot_first
    second_weight = block_second.astype(jnp.float32)
    first_weight = 1.0 - second_weight
    block_sum = jnp.sum(blocks, axis=1, dtype=jnp.float32)
    first_blocks = jnp.where(
        block_second[:, None, None], jnp.zeros((), jnp.bfloat16), blocks
    ).reshape(rows, width)
    last_blocks = jnp.where(
        block_second[:, None, None], blocks, jnp.zeros((), jnp.bfloat16)
    ).reshape(rows, width)
    part_sq_first = pack_sym(
        jnp.einsum("rd,re->de", first_blocks, first_blocks, preferred_element_type=jnp.float32)
    )
    part_sq_last = pack_sym(
        jnp.einsum("rd,re->de", last_blocks, last_blocks, preferred_element_type=jnp.float32)
    )
    part_sum_first = jnp.sum(first_weight[:, None] * block_sum, axis=0)
    part_sum_last = jnp.sum(second_weight[:, None] * block_sum, axis=0)
    right_sq = jnp.where(same_slide, part_sq_first, part_sq_last)
    right_sum = jnp.where(same_slide, part_sum_first, part_sum_last)
    zero_sq = jnp.zeros(part_sq_first.shape, jnp.float32)
    zero_sum = jnp.zeros((width,), jnp.float32)
    tail_sq, tail_sum, tail_flag = entering(
        (
            jnp.where(from_left, part_sq_first, 0.0),
            jnp.where(from_left, part_sum_first, 0.0),
            passing,
        ),
        "tile",
        add_chain,
        (zero_sq, zero_sum, jnp.float32(1.0)),
    )
    zero_q = jnp.zeros((width, width), jnp.bfloat16)
    zero_packed = jnp.zeros(part_sq_first.shape, jnp.bfloat16)
    owner_device = slide_offsets // rows
    owner_match = (
        owner_device[None, :] == jnp.arange(tile_count, dtype=jnp.int32)[:, None]
    ).astype(jnp.int32)
    owned_index = jnp.sum(owner_match * jnp.arange(slide_total, dtype=jnp.int32)[None, :], axis=1)
    outgoing = jnp.take(pooled_grad, owned_index, axis=0).reshape(width, width)
    grad_owned = lax.all_to_all(outgoing, "tile", split_axis=0, concat_axis=0, tiled=True)
    total_sq = unpack_sym(right_sq + tail_sq)
    total_sum = right_sum + tail_sum
    owned_q, owned_mean = lax.cond(
        owns,
        lambda: pool_backward(total_sq, total_sum, count_real[slot_last], grad_owned),
        lambda: (zero_q, zero_sum),
    )
    owned_packed = pack_sym(owned_q)
    given_packed, given_mean, given_flag = prefix(
        (owned_packed, owned_mean, passing),
        "tile",
        keep_nearest,
        (zero_packed, zero_sum, jnp.float32(1.0)),
    )
    given_q = unpack_sym(given_packed)
    q_first = jnp.where(from_left, given_q, owned_q)
    mean_first = jnp.where(from_left, given_mean, owned_mean)
    q_last = jnp.where(owns, owned_q, given_q)
    mean_last = jnp.where(owns, owned_mean, given_mean)
    first_grad = jnp.dot(first_blocks, q_first, preferred_element_type=jnp.float32)
    last_grad = jnp.dot(last_blocks, q_last, preferred_element_type=jnp.float32)
    row_second = jnp.repeat(second_weight, BLOCK)[:, None]
    row_mean = (1.0 - row_second) * mean_first[None, :] + row_second * mean_last[None, :]
    row_grad = jnp.where(valid[:, None], first_grad + last_grad + row_mean, 0.0).astype(
        jnp.bfloat16
    )
    feature_grad = jnp.einsum(
        "rd,kd->rk", row_grad, projection, preferred_element_type=jnp.float32
    ).astype(jnp.bfloat16)
    local_term = jnp.einsum("rk,rd->kd", features, row_grad, preferred_element_type=jnp.float32)
    projection_grad = reduce_everywhere(local_term)
    return (feature_grad, projection_grad)


def solution(mesh):
    placed = (P(("grp", "tile"), None), P(), P("grp", "tile", None), P("grp"), P("grp"))
    return jax.shard_map(
        shards,
        mesh=mesh,
        in_specs=placed,
        out_specs=(P(("grp", "tile"), None), P()),
        check_vma=False,
    )
```

```python
import functools

import jax
import jax.numpy as jnp
from jax import lax
from jax.experimental import pallas as pl
from jax.experimental.pallas import tpu as pltpu
from jax.sharding import PartitionSpec as P

BF = jnp.bfloat16
F32 = jnp.float32
ROWS = 256
PLANE = 4 * ROWS
DIN = 1024
D = 768
CHUNK = 256
CHUNKS = D // CHUNK
SLOTS = 6
PAIRS = [(i, j) for i in range(6) for j in range(i + 1)]
PAIRS = PAIRS + [(0, 0)] * (4 * SLOTS - len(PAIRS))
REAL = 21
MESSAGE = SLOTS * 128 + 16
VMEM = pl.BlockSpec(memory_space=pltpu.VMEM)
SMEM = pl.BlockSpec(memory_space=pltpu.SMEM)

BASE, OWN, FIRST, LAST, QUARTER, GRAD, EXTRA, PLACE = 48, 52, 54, 56, 58, 59, 60, 61

CORE_PAIRS = [(i, i ^ 1) for i in range(8)]


def x_shift(step):
    return [(x * 2 + c, (x + step) % 4 * 2 + c) for x in range(4) for c in range(2)]


def y_shift(step):
    return [(z * 4 + y, z * 4 + (y + step) % 4) for z in range(8) for y in range(4)]


def z_shift(step):
    return [(z * 4 + y, (z + step) % 8 * 4 + y) for z in range(8) for y in range(4)]


def y_to_ends(step):
    return [(z * 4 + (end - step) % 4, z * 4 + end) for z in range(8) for end in (0, 3)]


Z_GROUPS = [[z * 4 + y for z in range(8)] for y in range(4)]


def dot(a, b):
    return jnp.dot(a, b, preferred_element_type=F32)


def dot_rows(a, b):
    return lax.dot_general(a, b, (((0,), (0,)), ((), ())), preferred_element_type=F32)


def call(kernel, outs, specs, scratch=(), limit=32 << 20):
    return pl.pallas_call(
        kernel,
        out_shape=outs,
        in_specs=specs,
        out_specs=jax.tree.map(lambda _: VMEM, outs),
        scratch_shapes=list(scratch),
        compiler_params=pltpu.CompilerParams(vmem_limit_bytes=limit),
    )


def struct(shape, kind):
    return jax.ShapeDtypeStruct(shape, kind)


def part(index):
    return pl.ds(pl.multiple_of(index * 128, 128), 128)


def sums_kernel(info, x0, x1, x2, x3, first_out, last_out, local, local_row, own, first, last):
    for r, x in enumerate((x0, x1, x2, x3)):
        row = info[BASE + r] + lax.broadcasted_iota(jnp.int32, (ROWS, D), 0)
        here = pl.ds(r * ROWS, ROWS)
        value = x[...].astype(F32)
        for place, out in ((OWN, own), (FIRST, first), (LAST, last)):
            keep = (row >= info[place]) & (row < info[place + 1])
            out[here, :] = jnp.where(keep, value, 0.0).astype(BF)
    ones = jnp.ones((8, PLANE), BF)
    for c in range(CHUNKS):
        here = pl.ds(c * CHUNK, CHUNK)
        local[here, :] = dot_rows(own[:, here], own[...])
    local_row[...] = dot(ones, own[...])
    quarter = info[QUARTER]
    for source, out in ((first, first_out), (last, last_out)):
        for k in range(SLOTS):
            i = info[quarter * SLOTS + k]
            j = info[24 + quarter * SLOTS + k]
            block = dot_rows(source[:, part(i)], source[:, part(j)])
            block = jnp.where(quarter * SLOTS + k < REAL, block, 0.0)
            out[pl.ds(k * 128, 128), :] = block.astype(BF)
        total = dot(ones, source[...])
        high = total.astype(BF).astype(F32)
        low = total - high
        line = lax.broadcasted_iota(jnp.int32, (16, 128), 0)
        tail = jnp.zeros((16, 128), F32)
        for c in range(6):
            cut = slice(c * 128, (c + 1) * 128)
            tail = jnp.where(line == c, high[0:1, cut], tail)
            tail = jnp.where(line == 6 + c, low[0:1, cut], tail)
        out[pl.ds(SLOTS * 128, 16), :] = tail.astype(BF)


def half_kernel(grads, out):
    for i in range(CHUNKS):
        for j in range(i, CHUNKS):
            rows = pl.ds(i * CHUNK, CHUNK)
            cols = pl.ds(j * CHUNK, CHUNK)
            upper = grads[rows, cols].astype(F32)
            lower = grads[cols, rows].astype(F32)
            block = 0.5 * (upper + lower.T)
            out[rows, cols] = block
            if i != j:
                out[cols, rows] = block.T


def total_of(value):
    return jnp.sum(value, axis=(0, 1), keepdims=True)


def pool_kernel(
    info, number, local, local_row, e0, e1, e2, e3, half, x0, x1, x2, x3, f0, f1, f2, f3,
    sent, mine, g0, g1, g2, g3,
    covar, wide_a, wide_b, mean_col, mean_row, scaled_b, first_b, top_b, second_b, under_b, grad_b,
):
    count = number[0:1, 0:1]
    inverse = 1.0 / count
    covar[...] = local[...]
    mean_row[...] = local_row[...]

    @pl.when(info[EXTRA] > 0)
    def _():
        for r, extra in enumerate((e0, e1, e2, e3)):
            quarter = info[PLACE + r]
            for k in range(SLOTS):
                i = info[quarter * SLOTS + k]
                j = info[24 + quarter * SLOTS + k]
                block = extra[pl.ds(k * 128, 128), :].astype(F32)
                covar[part(i), part(j)] += block

                @pl.when(i != j)
                def _():
                    covar[part(j), part(i)] += block.T

        tail = e0[pl.ds(SLOTS * 128, 16), :].astype(F32)
        for c in range(6):
            cut = pl.ds(c * 128, 128)
            mean_row[:, cut] += tail[c : c + 1, :] + tail[6 + c : 7 + c, :]

    mean_row[...] = mean_row[...] * inverse
    mean_col[...] = mean_row[...].T
    squares = jnp.zeros((1, 1), F32)
    for c in range(CHUNKS):
        here = pl.ds(c * CHUNK, CHUNK)
        value = covar[here, :] * inverse - mean_col[here, 0:1] * mean_row[0:1, :]
        covar[here, :] = value
        squares += total_of(value * value)
    norm = jnp.sqrt(squares + 1e-6)
    over = 1.0 / norm
    root = jnp.sqrt(norm)
    for c in range(CHUNKS):
        here = pl.ds(c * CHUNK, CHUNK)
        scaled_b[here, :] = (covar[here, :] * over).astype(BF)
        top_b[here, :] = (half[here, :] * root).astype(BF)
    for c in range(CHUNKS):
        here = pl.ds(c * CHUNK, CHUNK)
        value = (1.5 * over) * covar[here, :] - 0.5 * dot(scaled_b[here, :], scaled_b[...])
        wide_a[here, :] = value
        first_b[here, :] = value.astype(BF)
    for c in range(CHUNKS):
        here = pl.ds(c * CHUNK, CHUNK)
        value = 1.5 * wide_a[here, :] - 0.5 * dot(scaled_b[here, :], first_b[...])
        second_b[here, :] = value.astype(BF)
        under_b[here, :] = dot(first_b[here, :], top_b[...]).astype(BF)
    sums = jnp.zeros((1, 1), F32)
    for c in range(CHUNKS):
        here = pl.ds(c * CHUNK, CHUNK)
        top = half[here, :] * root
        right = dot(top_b[here, :], second_b[...])
        sums += 1.5 * total_of(top * wide_a[here, :])
        sums -= 0.5 * total_of(right * first_b[here, :].astype(F32))
        value = 1.5 * top - 0.5 * (right + dot(second_b[here, :], top_b[...]))
        wide_b[here, :] = value
        grad_b[here, :] = value.astype(BF)
    inner = jnp.zeros((1, 1), F32)
    for c in range(CHUNKS):
        here = pl.ds(c * CHUNK, CHUNK)
        value = 1.5 * wide_b[here, :] + 0.25 * dot(under_b[here, :], first_b[...])
        value -= 0.5 * (dot(grad_b[here, :], scaled_b[...]) + dot(scaled_b[here, :], grad_b[...]))
        wide_a[here, :] = value
        inner += total_of(value * covar[here, :])
    grad_norm = sums * (0.5 * over) - inner * over * over
    scale = 2.0 * over * inverse
    mean_grad = jnp.zeros((1, D), F32)
    for c in range(CHUNKS):
        here = pl.ds(c * CHUNK, CHUNK)
        value = (wide_a[here, :] + grad_norm * covar[here, :]) * scale
        second_b[here, :] = value.astype(BF)
        mean_grad -= jnp.sum(value * mean_col[here, 0:1], axis=0, keepdims=True)
    for r, (x, g) in enumerate(((x0, g0), (x1, g1), (x2, g2), (x3, g3))):
        row = info[BASE + r] + lax.broadcasted_iota(jnp.int32, (ROWS, D), 0)
        keep = (row >= info[OWN]) & (row < info[GRAD])
        value = dot(x[...], second_b[...]) + mean_grad
        g[...] = jnp.where(keep, value, 0.0).astype(BF)
    core = info[PLACE + 4]
    for c in range(2):
        here = pl.ds(c * CHUNK, CHUNK)
        for place, out in ((1 - core, sent), (core, mine)):
            cols = pl.ds(pl.multiple_of(place * (DIN // 2) + c * CHUNK, CHUNK), CHUNK)
            value = dot_rows(f0[:, cols], g0[...])
            for f, g in ((f1, g1), (f2, g2), (f3, g3)):
                value += dot_rows(f[:, cols], g[...])
            out[here, :] = value.astype(out.dtype)


def split_kernel(place, mine, *refs):
    others, (own, *sends) = refs[: len(refs) - 4], refs[len(refs) - 4 :]
    rows = own.shape[0]

    def piece(step):
        here = pl.ds(pl.multiple_of(lax.rem(place[0] + step, 4) * rows, rows), rows)
        value = mine[here, :]
        for other in others:
            value = value + other[here, :].astype(F32)
        return value

    own[...] = piece(0)
    for step, out in zip((1, 3, 2), sends):
        out[...] = piece(step).astype(BF)


def add_kernel(mine, a, b, c, out):
    value = mine[...] + a[...].astype(F32) + b[...].astype(F32) + c[...].astype(F32)
    out[...] = value.astype(BF)


def sum_kernel(got, out):
    value = got[0].astype(F32)
    for z in range(1, 8):
        value = value + got[z].astype(F32)
    out[...] = value.astype(BF)


def join_kernel(place, own, a, b, c, out):
    rows = own.shape[0]
    for step, value in ((0, own), (1, a), (3, b), (2, c)):
        index = lax.rem(place[0] + 4 - step, 4)
        out[pl.ds(pl.multiple_of(index * rows, rows), rows), :] = value[...]


def final_kernel(core, own, other, out):
    rows = own.shape[0]
    out[pl.ds(pl.multiple_of(core[0] * rows, rows), rows), :] = own[...].astype(F32)
    out[pl.ds(pl.multiple_of((1 - core[0]) * rows, rows), rows), :] = other[...].astype(F32)


def three(values, axis, shift):
    return [lax.ppermute(v, axis, shift(step)) for step, v in zip((1, 3, 2), values)]


def reduce_everywhere(sent, mine, core, x_place, y_place):
    core, x_place, y_place = core[None], x_place[None], y_place[None]

    def pieces(rows):
        return [struct((rows, D), F32)] + [struct((rows, D), BF)] * 3

    got = lax.ppermute(sent, "grp", CORE_PAIRS)
    own, *sends = call(split_kernel, pieces(128), [SMEM, VMEM, VMEM])(x_place, mine, got)
    got = three(sends, "grp", x_shift)
    own, *sends = call(split_kernel, pieces(32), [SMEM] + [VMEM] * 4)(y_place, own, *got)
    got = three(sends, "tile", y_shift)
    value = call(add_kernel, struct((32, D), BF), [VMEM] * 4)(own, *got)
    value = jnp.broadcast_to(value[None], (8, 32, D))
    got = lax.all_to_all(value, "tile", 0, 0, axis_index_groups=Z_GROUPS, tiled=True)
    value = call(sum_kernel, struct((32, D), BF), [VMEM])(got)
    got = three([value] * 3, "tile", y_shift)
    value = call(join_kernel, struct((128, D), BF), [SMEM] + [VMEM] * 4)(y_place, value, *got)
    got = three([value] * 3, "grp", x_shift)
    value = call(join_kernel, struct((512, D), BF), [SMEM] + [VMEM] * 4)(x_place, value, *got)
    got = lax.ppermute(value, "grp", CORE_PAIRS)
    return call(final_kernel, struct((DIN, D), F32), [SMEM, VMEM, VMEM])(core, value, got)


def shards(features, projection, pooled_grad, slide_counts, slide_offsets):
    group = lax.axis_index("grp")
    tile = lax.axis_index("tile")
    core, x_place = group % 2, group // 2
    y, z = tile % 4, tile // 4
    total_rows = ROWS * lax.axis_size("tile")
    ends = jnp.concatenate([slide_offsets[1:], jnp.full((1,), total_rows, jnp.int32)])

    def slide_at(row):
        return jnp.sum((slide_offsets <= row[..., None]).astype(jnp.int32), axis=-1) - 1

    def of(array, index):
        ids = jnp.arange(array.shape[0], dtype=jnp.int32)
        return jnp.sum(jnp.where(ids == index[..., None], array, 0), axis=-1)

    def slide_for(tiles):
        at, plane = tiles % 4, tiles // 4
        first = slide_at(plane * PLANE)
        last = slide_at(plane * PLANE + PLANE - 1)
        inside = (at == 0) | (at == 3) & (last > first) | (first + at < last) & (at < 3)
        slide = jnp.where(at == 3, last, jnp.where(first + at < last, first + at, first))
        return slide, inside, first, last

    owned = slide_for(jnp.arange(32, dtype=jnp.int32))[0]
    outgoing = jnp.take(pooled_grad, owned, axis=0)
    grads = lax.all_to_all(outgoing, "tile", 0, 0, tiled=True).reshape(D, D)

    slide, inside, first, last = slide_for(tile)
    lo, hi = of(slide_offsets, slide), of(slide_offsets + slide_counts, slide)
    first_lo, first_hi = of(slide_offsets, first), of(slide_offsets + slide_counts, first)
    last_lo, last_hi = of(slide_offsets, last), of(slide_offsets + slide_counts, last)
    last_end = of(ends, last)
    quarters = jnp.stack([(y + 4 - r) % 4 for r in range(4)])
    scalars = [lo, hi, first_lo, first_hi, last_lo, last_hi, y, jnp.where(inside, hi, lo)]
    scalars = scalars + [((y == 0) | (y == 3)).astype(jnp.int32)]
    tables = jnp.array([i for i, _ in PAIRS] + [j for _, j in PAIRS], jnp.int32)
    info = jnp.concatenate(
        [tables, z * PLANE + quarters * ROWS, jnp.stack(scalars), quarters, core[None]]
    ).astype(jnp.int32)
    number = jnp.full((8, 128), of(slide_counts, slide).astype(F32))

    pieces = [features] + [lax.ppermute(features, "tile", y_shift(r)) for r in (1, 2, 3)]
    mixed = [dot(piece, projection).astype(BF) for piece in pieces]
    message = struct((MESSAGE, 128), BF)
    first_part, last_part, local, local_row = call(
        sums_kernel,
        [message, message, struct((D, D), F32), struct((8, D), F32)],
        [SMEM] + [VMEM] * 4,
        [pltpu.VMEM((PLANE, D), BF)] * 3,
    )(info, *mixed)

    start = z * PLANE
    left_1 = lax.ppermute(last_part, "tile", z_shift(1)).astype(F32)
    right_1 = lax.ppermute(first_part, "tile", z_shift(-1)).astype(F32)
    left_2 = lax.ppermute(last_part, "tile", z_shift(2)).astype(F32)
    right_2 = lax.ppermute(first_part, "tile", z_shift(-2)).astype(F32)
    before = jnp.where(first_lo < start, left_1, 0.0)
    before = before + jnp.where(first_lo < start - PLANE, left_2, 0.0)
    after = jnp.where(last_end > start + PLANE, right_1, 0.0)
    after = after + jnp.where(last_end > start + 2 * PLANE, right_2, 0.0)
    to_first = jnp.where(first == last, before + after, before).astype(BF)
    to_last = after.astype(BF)
    extras = [jnp.where(y == 0, to_first, to_last)]
    for step in (1, 2, 3):
        sending = jnp.where((y + step) % 4 == 0, to_first, to_last)
        extras.append(lax.ppermute(sending, "tile", y_to_ends(step)))

    half = call(half_kernel, struct((D, D), F32), [VMEM])(grads)
    wide = pltpu.VMEM((D, D), F32)
    narrow = pltpu.VMEM((D, D), BF)
    sent, mine, *row_grads = call(
        pool_kernel,
        [struct((512, D), BF), struct((512, D), F32)] + [struct((ROWS, D), BF)] * 4,
        [SMEM] + [VMEM] * 16,
        [wide] * 3 + [pltpu.VMEM((D, 8), F32), pltpu.VMEM((8, D), F32)] + [narrow] * 6,
        48 << 20,
    )(info, number, local, local_row, *extras, half, *mixed, *pieces)

    row_grad = row_grads[0]
    for r in (1, 2, 3):
        row_grad = row_grad + lax.ppermute(row_grads[r], "tile", y_shift(-r))
    projection_grad = reduce_everywhere(sent, mine, core, x_place, y)
    feature_grad = jnp.einsum(
        "rd,kd->rk", row_grad, projection, preferred_element_type=F32
    ).astype(BF)
    return (feature_grad, projection_grad)


def solution(mesh):
    placed = (P(("grp", "tile"), None), P(), P("grp", "tile", None), P("grp"), P("grp"))
    return jax.shard_map(
        shards,
        mesh=mesh,
        in_specs=placed,
        out_specs=(P(("grp", "tile"), None), P()),
        check_vma=False,
    )
```

```python
import functools

import jax
import jax.numpy as jnp
from jax import lax
from jax.experimental import pallas as pl
from jax.experimental.pallas import tpu as pltpu
from jax.sharding import PartitionSpec as P

BF = jnp.bfloat16
F32 = jnp.float32
ROWS = 256
PLANE = 4 * ROWS
DIN = 1024
D = 768
CHUNK = 256
CHUNKS = D // CHUNK
PAIRS = [(i, j) for i in range(6) for j in range(i + 1)]
STRIP = 32
TAIL = len(PAIRS) * STRIP
MESSAGE = TAIL + 16
VMEM = pl.BlockSpec(memory_space=pltpu.VMEM)
SMEM = pl.BlockSpec(memory_space=pltpu.SMEM)

BASE, OWN, FIRST, LAST, QUARTER, GRAD, EXTRA, END, ALONE, PLACE = 0, 4, 6, 8, 10, 11, 12, 13, 14, 15
COUNT, SCALARS = 20, 21

WORK = 5 * 10**9
CORE_PAIRS = [(i, i ^ 1) for i in range(8)]


def x_shift(step):
    return [(x * 2 + c, (x + step) % 4 * 2 + c) for x in range(4) for c in range(2)]


def y_shift(step):
    return [(z * 4 + y, z * 4 + (y + step) % 4) for z in range(8) for y in range(4)]


def z_shift(step):
    return [(z * 4 + y, (z + step) % 8 * 4 + y) for z in range(8) for y in range(4)]


def y_to_ends(step):
    return [(z * 4 + (end - step) % 4, z * 4 + end) for z in range(8) for end in (0, 3)]


def z_mirror(bits):
    return [(z * 4 + y, (z ^ bits) * 4 + y) for z in range(8) for y in range(4)]


def dot(a, b):
    return jnp.dot(a, b, preferred_element_type=F32)


def dot_rows(a, b):
    return lax.dot_general(a, b, (((0,), (0,)), ((), ())), preferred_element_type=F32)


def call(kernel, outs, specs, scratch=(), limit=16 << 20, work=None):
    cost = work and pl.CostEstimate(flops=work, bytes_accessed=10**7, transcendentals=0)
    return pl.pallas_call(
        kernel,
        out_shape=outs,
        in_specs=specs,
        out_specs=jax.tree.map(lambda _: VMEM, outs),
        scratch_shapes=list(scratch),
        cost_estimate=cost,
        compiler_params=pltpu.CompilerParams(vmem_limit_bytes=limit),
    )


def struct(shape, kind):
    return jax.ShapeDtypeStruct(shape, kind)


def plan_kernel(place, counts, offsets, grads, info, outgoing):
    total = offsets.shape[0]

    def slide_at(row):
        slide = jnp.int32(-1)
        for s in range(total):
            slide += (offsets[s] <= row).astype(jnp.int32)
        return slide

    def slide_for(at, first, last):
        inner = jnp.where(first + at < last, first + at, first)
        return jnp.where(at == 3, last, inner)

    def plan(plane, carry):
        first = slide_at(plane * PLANE)
        last = slide_at(plane * PLANE + PLANE - 1)
        for at in range(4):
            outgoing[plane * 4 + at] = grads[slide_for(at, first, last)]
        return carry

    lax.fori_loop(0, outgoing.shape[0] // 4, plan, 0)
    tile, core = place[0], place[1]
    y, z = lax.rem(tile, 4), lax.div(tile, 4)
    first, last = slide_at(z * PLANE), slide_at(z * PLANE + PLANE - 1)
    slide = slide_for(y, first, last)
    for start, index in ((OWN, slide), (FIRST, first), (LAST, last)):
        info[start] = offsets[index]
        info[start + 1] = offsets[index] + counts[index]
    for r in range(4):
        quarter = lax.rem(y + 4 - r, 4)
        info[BASE + r] = z * PLANE + quarter * ROWS
        info[PLACE + r] = quarter
    inside = (y == 0) | (y == 3) & (last > first) | (first + y < last) & (y < 3)
    after = offsets[jnp.minimum(last + 1, total - 1)]
    info[QUARTER] = y
    info[GRAD] = jnp.where(inside, info[OWN + 1], info[OWN])
    info[EXTRA] = ((y == 0) | (y == 3)).astype(jnp.int32)
    info[END] = jnp.where(last + 1 < total, after, outgoing.shape[0] * ROWS)
    info[ALONE] = (first == last).astype(jnp.int32)
    info[PLACE + 4] = core
    info[COUNT] = counts[slide]


def keep_rows(info, place, r, value):
    row = info[BASE + r] + lax.broadcasted_iota(jnp.int32, (ROWS, D), 0)
    keep = (row >= info[place]) & (row < info[place + 1])
    return jnp.where(keep, value, jnp.zeros((), BF))


def sums_kernel(info, x0, x1, x2, x3, first_out, last_out, first, last, strip):
    for r, x in enumerate((x0, x1, x2, x3)):
        value = x[...]
        here = pl.ds(r * ROWS, ROWS)
        first[here, :] = keep_rows(info, FIRST, r, value)
        last[here, :] = keep_rows(info, LAST, r, value)
    ones = jnp.ones((8, PLANE), BF)
    mine = pl.ds(pl.multiple_of(info[QUARTER] * STRIP, STRIP), STRIP)
    for source, out in ((first, first_out), (last, last_out)):
        slot = 0
        for i in range(6):
            width = (i + 1) * 128
            strip[:, 0:width] = dot_rows(source[:, i * 128 : width], source[:, 0:width])
            for j in range(i + 1):
                block = strip[mine, j * 128 : (j + 1) * 128]
                out[slot * STRIP : (slot + 1) * STRIP, :] = block.astype(BF)
                slot += 1
        total = dot(ones, source[...])
        high = total.astype(BF).astype(F32)
        low = total - high
        line = lax.broadcasted_iota(jnp.int32, (16, 128), 0)
        tail = jnp.zeros((16, 128), F32)
        for c in range(6):
            cut = slice(c * 128, (c + 1) * 128)
            tail = jnp.where(line == c, high[0:1, cut], tail)
            tail = jnp.where(line == 6 + c, low[0:1, cut], tail)
        out[TAIL:MESSAGE, :] = tail.astype(BF)


def local_kernel(info, x0, x1, x2, x3, local, local_row, own):
    for r, x in enumerate((x0, x1, x2, x3)):
        own[pl.ds(r * ROWS, ROWS), :] = keep_rows(info, OWN, r, x[...])
    for c in range(CHUNKS):
        here = pl.ds(c * CHUNK, CHUNK)
        local[here, :] = dot_rows(own[:, here], own[...])
    local_row[...] = dot(jnp.ones((8, PLANE), BF), own[...])


def flip_kernel(f0, f1, top, bottom, f3, out):
    start = 0
    for f in (f0, f1, top, bottom, f3):
        rows = f.shape[0]
        for c in range(DIN // CHUNK):
            here = pl.ds(c * CHUNK, CHUNK)
            out[here, start : start + rows] = f[:, here].astype(F32).T.astype(BF)
        start += rows


def fold_kernel(g1, g3, top, bottom, back, ahead):
    half = ROWS // 2
    back[0:half, :] = g1[0:half, :]
    back[half:ROWS, :] = g1[half:ROWS, :] + bottom[...]
    ahead[0:half, :] = g3[0:half, :] + top[...]
    ahead[half:ROWS, :] = g3[half:ROWS, :]


def extras_kernel(info, left_1, right_1, left_2, right_2, *outs):
    start = info[BASE] - info[QUARTER] * ROWS
    keeps = (
        info[FIRST] < start,
        info[END] > start + PLANE,
        info[FIRST] < start - PLANE,
        info[END] > start + 2 * PLANE,
    )
    values = [
        jnp.where(keep, value[...].astype(F32), 0.0)
        for keep, value in zip(keeps, (left_1, right_1, left_2, right_2))
    ]
    before = values[0] + values[2]
    after = values[1] + values[3]
    to_first = jnp.where(info[ALONE] > 0, before + after, before).astype(BF)
    to_last = after.astype(BF)
    for step, out in enumerate(outs):
        last = lax.rem(info[QUARTER] + step, 4) == 3

        @pl.when(last)
        def _():
            out[...] = to_last

        @pl.when(jnp.logical_not(last))
        def _():
            out[...] = to_first


def half_kernel(grads, out):
    for i in range(CHUNKS):
        for j in range(i, CHUNKS):
            rows = pl.ds(i * CHUNK, CHUNK)
            cols = pl.ds(j * CHUNK, CHUNK)
            upper = grads[rows, cols].astype(F32)
            lower = grads[cols, rows].astype(F32)
            block = 0.5 * (upper + lower.T)
            out[rows, cols] = block
            if i != j:
                out[cols, rows] = block.T


def total_of(value):
    return jnp.sum(value, axis=(0, 1), keepdims=True)


def pool_kernel(
    info, local, local_row, e0, e1, e2, e3, half, x0, x1, x2, x3, g0, g1, g2, g3,
    blocks, covar, wide_a, wide_b, mean_col, mean_row, scaled_b, first_b, top_b, second_b, under_b, grad_b,
):
    inverse = 1.0 / jnp.full((1, 1), info[COUNT], jnp.int32).astype(F32)
    covar[...] = local[...]
    mean_row[...] = local_row[...]

    @pl.when(info[EXTRA] > 0)
    def _():
        for r, extra in enumerate((e0, e1, e2, e3)):
            for slot in range(len(PAIRS)):
                row = pl.multiple_of(slot * 128 + info[PLACE + r] * STRIP, STRIP)
                piece = extra[slot * STRIP : (slot + 1) * STRIP, :]
                blocks[pl.ds(row, STRIP), :] = piece.astype(F32)
        for slot, (i, j) in enumerate(PAIRS):
            block = blocks[slot * 128 : (slot + 1) * 128, :]
            rows, cols = pl.ds(i * 128, 128), pl.ds(j * 128, 128)
            covar[rows, cols] += block
            if i != j:
                covar[cols, rows] += block.T

        tail = e0[TAIL:MESSAGE, :].astype(F32)
        for c in range(6):
            cut = pl.ds(c * 128, 128)
            mean_row[:, cut] += tail[c : c + 1, :] + tail[6 + c : 7 + c, :]

    mean_row[...] = mean_row[...] * inverse
    mean_col[...] = mean_row[...].T
    squares = jnp.zeros((1, 1), F32)
    for c in range(CHUNKS):
        here = pl.ds(c * CHUNK, CHUNK)
        value = covar[here, :] * inverse - mean_col[here, 0:1] * mean_row[0:1, :]
        covar[here, :] = value
        squares += total_of(value * value)
    norm = jnp.sqrt(squares + 1e-6)
    over = 1.0 / norm
    root = jnp.sqrt(norm)
    for c in range(CHUNKS):
        here = pl.ds(c * CHUNK, CHUNK)
        scaled_b[here, :] = (covar[here, :] * over).astype(BF)
        top_b[here, :] = (half[here, :] * root).astype(BF)
    for c in range(CHUNKS):
        here = pl.ds(c * CHUNK, CHUNK)
        value = (1.5 * over) * covar[here, :] - 0.5 * dot(scaled_b[here, :], scaled_b[...])
        wide_a[here, :] = value
        first_b[here, :] = value.astype(BF)
    for c in range(CHUNKS):
        here = pl.ds(c * CHUNK, CHUNK)
        value = 1.5 * wide_a[here, :] - 0.5 * dot(scaled_b[here, :], first_b[...])
        second_b[here, :] = value.astype(BF)
        under_b[here, :] = dot(first_b[here, :], top_b[...]).astype(BF)
    sums = jnp.zeros((1, 1), F32)
    for c in range(CHUNKS):
        here = pl.ds(c * CHUNK, CHUNK)
        top = half[here, :] * root
        right = dot(top_b[here, :], second_b[...])
        sums += 1.5 * total_of(top * wide_a[here, :])
        sums -= 0.5 * total_of(right * first_b[here, :].astype(F32))
        value = 1.5 * top - 0.5 * (right + dot(second_b[here, :], top_b[...]))
        wide_b[here, :] = value
        grad_b[here, :] = value.astype(BF)
    inner = jnp.zeros((1, 1), F32)
    for c in range(CHUNKS):
        here = pl.ds(c * CHUNK, CHUNK)
        value = 1.5 * wide_b[here, :] + 0.25 * dot(under_b[here, :], first_b[...])
        value -= 0.5 * (dot(grad_b[here, :], scaled_b[...]) + dot(scaled_b[here, :], grad_b[...]))
        wide_a[here, :] = value
        inner += total_of(value * covar[here, :])
    grad_norm = sums * (0.5 * over) - inner * over * over
    scale = 2.0 * over * inverse
    mean_grad = jnp.zeros((1, D), F32)
    for c in range(CHUNKS):
        here = pl.ds(c * CHUNK, CHUNK)
        value = (wide_a[here, :] + grad_norm * covar[here, :]) * scale
        second_b[here, :] = value.astype(BF)
        mean_grad -= jnp.sum(value * mean_col[here, 0:1], axis=0, keepdims=True)
    for r, (x, g) in enumerate(((x0, g0), (x1, g1), (x2, g2), (x3, g3))):
        row = info[BASE + r] + lax.broadcasted_iota(jnp.int32, (ROWS, D), 0)
        keep = (row >= info[OWN]) & (row < info[GRAD])
        value = dot(x[...], second_b[...]) + mean_grad
        g[...] = jnp.where(keep, value, 0.0).astype(BF)


def term_kernel(info, g0, g1, g2, g3, flipped, sent, mine):
    core = info[PLACE + 4]
    half = DIN // 2
    for place, out in ((1 - core, sent), (core, mine)):
        for c in range(half // CHUNK):
            here = pl.ds(pl.multiple_of(place * half + c * CHUNK, CHUNK), CHUNK)
            value = dot(flipped[here, 0:ROWS], g0[...])
            for r, g in ((1, g1), (2, g2), (3, g3)):
                value += dot(flipped[here, r * ROWS : (r + 1) * ROWS], g[...])
            out[c * CHUNK : (c + 1) * CHUNK, :] = value.astype(out.dtype)


def split_kernel(place, mine, *refs):
    others, (own, *sends) = refs[: len(refs) - 4], refs[len(refs) - 4 :]
    rows = own.shape[0]

    def piece(step):
        here = pl.ds(pl.multiple_of(lax.rem(place[0] + step, 4) * rows, rows), rows)
        value = mine[here, :]
        for other in others:
            value = value + other[here, :].astype(F32)
        return value

    own[...] = piece(0)
    for step, out in zip((1, 3, 2), sends):
        out[...] = piece(step).astype(BF)


def add_kernel(mine, a, b, c, out):
    value = mine[...] + a[...].astype(F32) + b[...].astype(F32) + c[...].astype(F32)
    out[...] = value.astype(BF)


def four_kernel(own, a, b, c, out):
    near = own[...].astype(F32) + a[...].astype(F32)
    out[...] = (near + (b[...].astype(F32) + c[...].astype(F32))).astype(BF)


def two_kernel(own, other, out):
    out[...] = (own[...].astype(F32) + other[...].astype(F32)).astype(BF)


def join_kernel(place, own, a, b, c, out):
    rows = own.shape[0]
    for step, value in ((0, own), (1, a), (3, b), (2, c)):
        index = lax.rem(place[0] + 4 - step, 4)
        out[pl.ds(pl.multiple_of(index * rows, rows), rows), :] = value[...]


def final_kernel(core, own, other, out):
    rows = own.shape[0]
    out[pl.ds(pl.multiple_of(core[0] * rows, rows), rows), :] = own[...].astype(F32)
    out[pl.ds(pl.multiple_of((1 - core[0]) * rows, rows), rows), :] = other[...].astype(F32)


def three(values, axis, shift):
    return [lax.ppermute(v, axis, shift(step)) for step, v in zip((1, 3, 2), values)]


def reduce_everywhere(sent, mine, row_grads, core, x_place, y_place):
    half_rows = ROWS // 2
    g0, g1, g2, g3 = row_grads
    top = lax.ppermute(g2[:half_rows], "tile", y_shift(1))
    bottom = lax.ppermute(g2[half_rows:], "tile", y_shift(-1))
    core, x_place, y_place = core[None], x_place[None], y_place[None]

    def pieces(rows):
        return [struct((rows, D), F32)] + [struct((rows, D), BF)] * 3

    got = lax.ppermute(sent, "grp", CORE_PAIRS)
    own, *sends = call(split_kernel, pieces(128), [SMEM, VMEM, VMEM])(x_place, mine, got)
    got = three(sends, "grp", x_shift)
    own, *sends = call(split_kernel, pieces(32), [SMEM] + [VMEM] * 4)(y_place, own, *got)
    got = three(sends, "tile", y_shift)
    got, top, bottom = lax.optimization_barrier((got, top, bottom))
    value = call(add_kernel, struct((32, D), BF), [VMEM] * 4)(own, *got)
    back, ahead = call(fold_kernel, [struct((ROWS, D), BF)] * 2, [VMEM] * 4)(g1, g3, top, bottom)
    home = [lax.ppermute(back, "tile", y_shift(-1)), lax.ppermute(ahead, "tile", y_shift(1))]
    got = [lax.ppermute(value, "tile", z_mirror(bits)) for bits in (1, 2, 3)]
    value = call(four_kernel, struct((32, D), BF), [VMEM] * 4)(value, *got)
    got = lax.ppermute(value, "tile", z_mirror(4))
    value = call(two_kernel, struct((32, D), BF), [VMEM] * 2)(value, got)
    value, home = lax.optimization_barrier((value, home))
    got = three([value] * 3, "tile", y_shift)
    value = call(join_kernel, struct((128, D), BF), [SMEM] + [VMEM] * 4)(y_place, value, *got)
    got = three([value] * 3, "grp", x_shift)
    value = call(join_kernel, struct((512, D), BF), [SMEM] + [VMEM] * 4)(x_place, value, *got)
    got = lax.ppermute(value, "grp", CORE_PAIRS)
    return call(final_kernel, struct((DIN, D), F32), [SMEM, VMEM, VMEM])(core, value, got), g0 + home[0] + home[1]


def shards(features, projection, pooled_grad, slide_counts, slide_offsets):
    group = lax.axis_index("grp")
    tile = lax.axis_index("tile")
    core, x_place = group % 2, group // 2
    y = tile % 4
    tiles = lax.axis_size("tile")
    info, outgoing = pl.pallas_call(
        plan_kernel,
        out_shape=[
            struct((SCALARS,), jnp.int32),
            struct((tiles,) + pooled_grad.shape[1:], BF),
        ],
        in_specs=[SMEM] * 3 + [VMEM],
        out_specs=[SMEM, VMEM],
        compiler_params=pltpu.CompilerParams(vmem_limit_bytes=16 << 20),
    )(jnp.stack([tile, core]).astype(jnp.int32), slide_counts, slide_offsets, pooled_grad)
    grads = lax.all_to_all(outgoing, "tile", 0, 0, tiled=True).reshape(D, D)

    half_rows = ROWS // 2
    behind = lax.ppermute(features, "tile", y_shift(1))
    ahead = lax.ppermute(features, "tile", y_shift(-1))
    top = lax.ppermute(behind[:half_rows], "tile", y_shift(1))
    bottom = lax.ppermute(ahead[half_rows:], "tile", y_shift(-1))
    across = jnp.concatenate([top, bottom], axis=0)
    mixed = [dot(piece, projection).astype(BF) for piece in (features, behind, across, ahead)]
    message = struct((MESSAGE, 128), BF)
    first_part, last_part = call(
        sums_kernel,
        [message, message],
        [SMEM] + [VMEM] * 4,
        [pltpu.VMEM((PLANE, D), BF)] * 2 + [pltpu.VMEM((128, D), F32)],
        work=WORK,
    )(info, *mixed)
    local, local_row = call(
        local_kernel,
        [struct((D, D), F32), struct((8, D), F32)],
        [SMEM] + [VMEM] * 4,
        [pltpu.VMEM((PLANE, D), BF)],
        work=WORK,
    )(info, *mixed)
    flipped = call(flip_kernel, struct((DIN, PLANE), BF), [VMEM] * 5, work=WORK)(
        features, behind, top, bottom, ahead
    )

    around = [
        lax.ppermute(last_part, "tile", z_shift(1)),
        lax.ppermute(first_part, "tile", z_shift(-1)),
        lax.ppermute(last_part, "tile", z_shift(2)),
        lax.ppermute(first_part, "tile", z_shift(-2)),
    ]
    half = call(half_kernel, struct((D, D), F32), [VMEM])(grads)
    half, *around = lax.optimization_barrier((half, *around))
    extras = call(extras_kernel, [message] * 4, [SMEM] + [VMEM] * 4, work=WORK)(info, *around)
    extras = list(extras[:1]) + [
        lax.ppermute(extra, "tile", y_to_ends(step)) for step, extra in zip((1, 2, 3), extras[1:])
    ]

    wide = pltpu.VMEM((D, D), F32)
    narrow = pltpu.VMEM((D, D), BF)
    row_grads = call(
        pool_kernel,
        [struct((ROWS, D), BF)] * 4,
        [SMEM] + [VMEM] * 11,
        [pltpu.VMEM((len(PAIRS) * 128, 128), F32)] + [wide] * 3 + [pltpu.VMEM((D, 8), F32), pltpu.VMEM((8, D), F32)] + [narrow] * 6,
        26 << 20,
        WORK,
    )(info, local, local_row, *extras, half, *mixed)
    sent, mine = call(
        term_kernel,
        [struct((512, D), BF), struct((512, D), F32)],
        [SMEM] + [VMEM] * 5,
        work=WORK,
    )(info, *row_grads, flipped)

    projection_grad, row_grad = reduce_everywhere(sent, mine, row_grads, core, x_place, y)
    feature_grad = jnp.einsum(
        "rd,kd->rk", row_grad, projection, preferred_element_type=F32
    ).astype(BF)
    return (feature_grad, projection_grad)


def solution(mesh):
    placed = (P(("grp", "tile"), None), P(), P("grp", "tile", None), P("grp"), P("grp"))
    return jax.shard_map(
        shards,
        mesh=mesh,
        in_specs=placed,
        out_specs=(P(("grp", "tile"), None), P()),
        check_vma=False,
    )
```

```python
import functools

import jax
import jax.numpy as jnp
from jax import lax
from jax.experimental import pallas as pl
from jax.experimental.pallas import tpu as pltpu
from jax.sharding import PartitionSpec as P

BF = jnp.bfloat16
F32 = jnp.float32
ROWS = 256
PLANE = 4 * ROWS
DIN = 1024
D = 768
CHUNK = 256
CHUNKS = D // CHUNK
PAIRS = [(i, j) for i in range(6) for j in range(i + 1)]
STRIP = 32
TAIL = len(PAIRS) * STRIP
MESSAGE = TAIL + 16
PIECES = ((0, 0, ROWS), (1, 0, ROWS), (2, 0, ROWS // 2), (2, ROWS // 2, ROWS // 2), (3, 0, ROWS))
VMEM = pl.BlockSpec(memory_space=pltpu.VMEM)
SMEM = pl.BlockSpec(memory_space=pltpu.SMEM)

BASE, OWN, FIRST, LAST, QUARTER, GRAD, EXTRA, END, ALONE, PLACE = 0, 4, 6, 8, 10, 11, 12, 13, 14, 15
COUNT, SCALARS = 20, 21

WORK = 5 * 10**9
CORE_PAIRS = [(i, i ^ 1) for i in range(8)]


def x_shift(step):
    return [(x * 2 + c, (x + step) % 4 * 2 + c) for x in range(4) for c in range(2)]


def y_shift(step):
    return [(z * 4 + y, z * 4 + (y + step) % 4) for z in range(8) for y in range(4)]


def z_shift(step):
    return [(z * 4 + y, (z + step) % 8 * 4 + y) for z in range(8) for y in range(4)]


def y_to_ends(step):
    return [(z * 4 + (end - step) % 4, z * 4 + end) for z in range(8) for end in (0, 3)]


def z_across():
    pair = (6, 7, 4, 5, 2, 3, 0, 1)
    return [(z * 4 + y, pair[z] * 4 + y) for z in range(8) for y in range(4)]


def z_mirror(bits):
    return [(z * 4 + y, (z ^ bits) * 4 + y) for z in range(8) for y in range(4)]


def dot(a, b):
    return jnp.dot(a, b, preferred_element_type=F32)


def dot_rows(a, b):
    return lax.dot_general(a, b, (((0,), (0,)), ((), ())), preferred_element_type=F32)


def call(kernel, outs, specs, scratch=(), limit=16 << 20, work=None):
    cost = work and pl.CostEstimate(flops=work, bytes_accessed=10**7, transcendentals=0)
    return pl.pallas_call(
        kernel,
        out_shape=outs,
        in_specs=specs,
        out_specs=jax.tree.map(lambda _: VMEM, outs),
        scratch_shapes=list(scratch),
        cost_estimate=cost,
        compiler_params=pltpu.CompilerParams(vmem_limit_bytes=limit),
    )


def struct(shape, kind):
    return jax.ShapeDtypeStruct(shape, kind)


def plan_kernel(place, counts, offsets, grads, info, outgoing):
    total = offsets.shape[0]

    def slide_at(row):
        slide = jnp.int32(-1)
        for s in range(total):
            slide += (offsets[s] <= row).astype(jnp.int32)
        return slide

    def slide_for(at, first, last):
        inner = jnp.where(first + at < last, first + at, first)
        return jnp.where(at == 3, last, inner)

    def plan(plane, carry):
        first = slide_at(plane * PLANE)
        last = slide_at(plane * PLANE + PLANE - 1)
        for at in range(4):
            outgoing[plane * 4 + at] = grads[slide_for(at, first, last)]
        return carry

    lax.fori_loop(0, outgoing.shape[0] // 4, plan, 0)
    tile, core = place[0], place[1]
    y, z = lax.rem(tile, 4), lax.div(tile, 4)
    first, last = slide_at(z * PLANE), slide_at(z * PLANE + PLANE - 1)
    slide = slide_for(y, first, last)
    for start, index in ((OWN, slide), (FIRST, first), (LAST, last)):
        info[start] = offsets[index]
        info[start + 1] = offsets[index] + counts[index]
    for r in range(4):
        quarter = lax.rem(y + 4 - r, 4)
        info[BASE + r] = z * PLANE + quarter * ROWS
        info[PLACE + r] = quarter
    inside = (y == 0) | (y == 3) & (last > first) | (first + y < last) & (y < 3)
    after = offsets[jnp.minimum(last + 1, total - 1)]
    info[QUARTER] = y
    info[GRAD] = jnp.where(inside, info[OWN + 1], info[OWN])
    info[EXTRA] = ((y == 0) | (y == 3)).astype(jnp.int32)
    info[END] = jnp.where(last + 1 < total, after, outgoing.shape[0] * ROWS)
    info[ALONE] = (first == last).astype(jnp.int32)
    info[PLACE + 4] = core
    info[COUNT] = counts[slide]


def keep_rows(info, place, r, skip, rows, lanes):
    row = info[BASE + r] + skip + lax.broadcasted_iota(jnp.int32, (rows, lanes), 0)
    return (row >= info[place]) & (row < info[place + 1])


def store_kept(keep, x, out, start):
    rows = x.shape[0]
    for c in range(6):
        cols = slice(c * 128, (c + 1) * 128)
        out[start : start + rows, cols] = jnp.where(keep, x[:, cols], jnp.zeros((), BF))


def sums_kernel(info, x0, x1, top, bottom, x3, first_out, last_out, both, strips):
    line = lax.broadcasted_iota(jnp.int32, (1, PLANE), 1)
    place = jnp.zeros((1, PLANE), jnp.int32)
    for (r, skip, rows), x in zip(PIECES, (x0, x1, top, bottom, x3)):
        keep = keep_rows(info, FIRST, r, skip, rows, 128)
        keep = keep | keep_rows(info, LAST, r, skip, rows, 128)
        store_kept(keep, x, both, r * ROWS + skip)
        inside = (line >= r * ROWS + skip) & (line < r * ROWS + skip + rows)
        place = jnp.where(inside, line - r * ROWS + info[BASE + r], place)
    row = lax.broadcasted_iota(jnp.int32, (6 * STRIP, D), 0)
    col = lax.broadcasted_iota(jnp.int32, (6 * STRIP, D), 1)
    wanted = (row >> 5) * 128 + (row & (STRIP - 1)) + info[QUARTER] * STRIP
    select = jnp.where(col == wanted, 1.0, 0.0).astype(BF)
    chosen = lax.dot_general(
        select, both[...], (((1,), (1,)), ((), ())), preferred_element_type=F32
    )
    for start, out in ((FIRST, first_out), (LAST, last_out)):
        keep = (place >= info[start]) & (place < info[start + 1])
        kept = jnp.where(keep, chosen, 0.0).astype(BF)
        ones = jnp.broadcast_to(jnp.where(keep, 1.0, 0.0), (16, PLANE)).astype(BF)
        strips[...] = dot(jnp.concatenate([kept, ones], axis=0), both[...])
        for slot, (i, j) in enumerate(PAIRS):
            block = strips[i * STRIP : (i + 1) * STRIP, j * 128 : (j + 1) * 128]
            out[slot * STRIP : (slot + 1) * STRIP, :] = block.astype(BF)
        total = strips[6 * STRIP : 6 * STRIP + 8, :]
        high = total.astype(BF).astype(F32)
        low = total - high
        count = lax.broadcasted_iota(jnp.int32, (16, 128), 0)
        tail = jnp.zeros((16, 128), F32)
        for c in range(6):
            cut = slice(c * 128, (c + 1) * 128)
            tail = jnp.where(count == c, high[0:1, cut], tail)
            tail = jnp.where(count == 6 + c, low[0:1, cut], tail)
        out[TAIL:MESSAGE, :] = tail.astype(BF)


def local_kernel(info, x0, x1, top, bottom, x3, local, local_row, own):
    for (r, skip, rows), x in zip(PIECES, (x0, x1, top, bottom, x3)):
        store_kept(keep_rows(info, OWN, r, skip, rows, 128), x, own, r * ROWS + skip)
    for c in range(CHUNKS):
        here = pl.ds(c * CHUNK, CHUNK)
        local[here, :] = dot_rows(own[:, here], own[...])
    local_row[...] = dot(jnp.ones((8, PLANE), BF), own[...])


def flip_kernel(f0, f1, top, bottom, f3, out):
    start = 0
    for f in (f0, f1, top, bottom, f3):
        rows = f.shape[0]
        for c in range(DIN // CHUNK):
            here = pl.ds(c * CHUNK, CHUNK)
            out[here, start : start + rows] = f[:, here].astype(F32).T.astype(BF)
        start += rows


def fold_kernel(g1, g3, top, bottom, back, ahead):
    half = ROWS // 2
    back[0:half, :] = g1[0:half, :]
    back[half:ROWS, :] = g1[half:ROWS, :] + bottom[...]
    ahead[0:half, :] = g3[0:half, :] + top[...]
    ahead[half:ROWS, :] = g3[half:ROWS, :]


def extras_kernel(info, left_1, right_1, left_2, right_2, *outs):
    start = info[BASE] - info[QUARTER] * ROWS
    keeps = (
        info[FIRST] < start,
        info[END] > start + PLANE,
        info[FIRST] < start - PLANE,
        info[END] > start + 2 * PLANE,
    )
    values = [
        jnp.where(keep, value[...].astype(F32), 0.0)
        for keep, value in zip(keeps, (left_1, right_1, left_2, right_2))
    ]
    before = values[0] + values[2]
    after = values[1] + values[3]
    to_first = jnp.where(info[ALONE] > 0, before + after, before).astype(BF)
    to_last = after.astype(BF)
    for step, out in enumerate(outs):
        last = lax.rem(info[QUARTER] + step, 4) == 3

        @pl.when(last)
        def _():
            out[...] = to_last

        @pl.when(jnp.logical_not(last))
        def _():
            out[...] = to_first


def half_kernel(grads, out):
    for i in range(CHUNKS):
        for j in range(i, CHUNKS):
            rows = pl.ds(i * CHUNK, CHUNK)
            cols = pl.ds(j * CHUNK, CHUNK)
            upper = grads[rows, cols].astype(F32)
            lower = grads[cols, rows].astype(F32)
            block = 0.5 * (upper + lower.T)
            out[rows, cols] = block
            if i != j:
                out[cols, rows] = block.T


def total_of(value):
    return jnp.sum(value, axis=(0, 1), keepdims=True)


def pool_kernel(
    info, local, local_row, e0, e1, e2, e3, half, x0, x1, xt, xb, x3, g0, g1, gt, gb, g3,
    blocks, covar, wide_a, wide_b, mean_col, mean_row, scaled_b, first_b, top_b, second_b, under_b, grad_b,
):
    inverse = 1.0 / jnp.full((1, 1), info[COUNT], jnp.int32).astype(F32)
    covar[...] = local[...]
    mean_row[...] = local_row[...]

    @pl.when(info[EXTRA] > 0)
    def _():
        for r, extra in enumerate((e0, e1, e2, e3)):
            for slot in range(len(PAIRS)):
                row = pl.multiple_of(slot * 128 + info[PLACE + r] * STRIP, STRIP)
                piece = extra[slot * STRIP : (slot + 1) * STRIP, :]
                blocks[pl.ds(row, STRIP), :] = piece.astype(F32)
        for slot, (i, j) in enumerate(PAIRS):
            block = blocks[slot * 128 : (slot + 1) * 128, :]
            rows, cols = pl.ds(i * 128, 128), pl.ds(j * 128, 128)
            covar[rows, cols] += block
            if i != j:
                covar[cols, rows] += block.T

        tail = e0[TAIL:MESSAGE, :].astype(F32)
        for c in range(6):
            cut = pl.ds(c * 128, 128)
            mean_row[:, cut] += tail[c : c + 1, :] + tail[6 + c : 7 + c, :]

    mean_row[...] = mean_row[...] * inverse
    mean_col[...] = mean_row[...].T
    squares = jnp.zeros((1, 1), F32)
    for c in range(CHUNKS):
        here = pl.ds(c * CHUNK, CHUNK)
        value = covar[here, :] * inverse - mean_col[here, 0:1] * mean_row[0:1, :]
        covar[here, :] = value
        squares += total_of(value * value)
    norm = jnp.sqrt(squares + 1e-6)
    over = 1.0 / norm
    root = jnp.sqrt(norm)
    for c in range(CHUNKS):
        here = pl.ds(c * CHUNK, CHUNK)
        scaled_b[here, :] = (covar[here, :] * over).astype(BF)
        top_b[here, :] = (half[here, :] * root).astype(BF)
    for c in range(CHUNKS):
        here = pl.ds(c * CHUNK, CHUNK)
        value = (1.5 * over) * covar[here, :] - 0.5 * dot(scaled_b[here, :], scaled_b[...])
        wide_a[here, :] = value
        first_b[here, :] = value.astype(BF)
    for c in range(CHUNKS):
        here = pl.ds(c * CHUNK, CHUNK)
        value = 1.5 * wide_a[here, :] - 0.5 * dot(scaled_b[here, :], first_b[...])
        second_b[here, :] = value.astype(BF)
        under_b[here, :] = dot(first_b[here, :], top_b[...]).astype(BF)
    sums = jnp.zeros((1, 1), F32)
    for c in range(CHUNKS):
        here = pl.ds(c * CHUNK, CHUNK)
        top = half[here, :] * root
        right = dot(top_b[here, :], second_b[...])
        sums += 1.5 * total_of(top * wide_a[here, :])
        sums -= 0.5 * total_of(right * first_b[here, :].astype(F32))
        value = 1.5 * top - 0.5 * (right + dot(second_b[here, :], top_b[...]))
        wide_b[here, :] = value
        grad_b[here, :] = value.astype(BF)
    inner = jnp.zeros((1, 1), F32)
    for c in range(CHUNKS):
        here = pl.ds(c * CHUNK, CHUNK)
        value = 1.5 * wide_b[here, :] + 0.25 * dot(under_b[here, :], first_b[...])
        value -= 0.5 * (dot(grad_b[here, :], scaled_b[...]) + dot(scaled_b[here, :], grad_b[...]))
        wide_a[here, :] = value
        inner += total_of(value * covar[here, :])
    grad_norm = sums * (0.5 * over) - inner * over * over
    scale = 2.0 * over * inverse
    mean_grad = jnp.zeros((1, D), F32)
    for c in range(CHUNKS):
        here = pl.ds(c * CHUNK, CHUNK)
        value = (wide_a[here, :] + grad_norm * covar[here, :]) * scale
        second_b[here, :] = value.astype(BF)
        mean_grad -= jnp.sum(value * mean_col[here, 0:1], axis=0, keepdims=True)
    xs, gs = (x0, x1, xt, xb, x3), (g0, g1, gt, gb, g3)
    for (r, skip, rows), x, g in zip(PIECES, xs, gs):
        row = info[BASE + r] + skip + lax.broadcasted_iota(jnp.int32, (rows, D), 0)
        keep = (row >= info[OWN]) & (row < info[GRAD])
        value = dot(x[...], second_b[...]) + mean_grad
        g[...] = jnp.where(keep, value, 0.0).astype(BF)


def term_kernel(info, g0, g1, gt, gb, g3, flipped, sent, mine, plane):
    for (r, skip, rows), g in zip(PIECES, (g0, g1, gt, gb, g3)):
        plane[r * ROWS + skip : r * ROWS + skip + rows, :] = g[...]
    core = info[PLACE + 4]
    half = DIN // 2
    for place, out in ((1 - core, sent), (core, mine)):
        for c in range(half // CHUNK):
            here = pl.ds(pl.multiple_of(place * half + c * CHUNK, CHUNK), CHUNK)
            value = dot(flipped[here, :], plane[...])
            out[c * CHUNK : (c + 1) * CHUNK, :] = value.astype(out.dtype)


def split_kernel(place, mine, *refs):
    others, (own, *sends) = refs[: len(refs) - 4], refs[len(refs) - 4 :]
    rows = own.shape[0]

    def piece(step):
        here = pl.ds(pl.multiple_of(lax.rem(place[0] + step, 4) * rows, rows), rows)
        value = mine[here, :].astype(F32)
        for other in others:
            value = value + other[here, :].astype(F32)
        return value

    own[...] = piece(0)
    for step, out in zip((1, 3, 2), sends):
        out[...] = piece(step).astype(BF)


def add_kernel(mine, a, b, c, out):
    value = mine[...] + a[...].astype(F32) + b[...].astype(F32) + c[...].astype(F32)
    out[...] = value.astype(BF)


def four_kernel(own, a, b, c, out):
    near = own[...].astype(F32) + a[...].astype(F32)
    out[...] = (near + (b[...].astype(F32) + c[...].astype(F32))).astype(BF)


def two_kernel(own, other, out):
    out[...] = (own[...].astype(F32) + other[...].astype(F32)).astype(BF)


def join_kernel(place, own, a, b, c, out):
    rows = own.shape[0]
    for step, value in ((0, own), (1, a), (3, b), (2, c)):
        index = lax.rem(place[0] + 4 - step, 4)
        out[pl.ds(pl.multiple_of(index * rows, rows), rows), :] = value[...]


def final_kernel(core, own, other, out):
    rows = own.shape[0]
    out[pl.ds(pl.multiple_of(core[0] * rows, rows), rows), :] = own[...].astype(F32)
    out[pl.ds(pl.multiple_of((1 - core[0]) * rows, rows), rows), :] = other[...].astype(F32)


def three(values, axis, shift):
    return [lax.ppermute(v, axis, shift(step)) for step, v in zip((1, 3, 2), values)]


def reduce_everywhere(sent, mine, row_grads, core, x_place, y_place):
    g0, g1, top, bottom, g3 = row_grads
    top = lax.ppermute(top, "tile", y_shift(1))
    bottom = lax.ppermute(bottom, "tile", y_shift(-1))
    core, x_place, y_place = core[None], x_place[None], y_place[None]

    def pieces(rows):
        return [struct((rows, D), F32)] + [struct((rows, D), BF)] * 3

    got = lax.ppermute(sent, "grp", CORE_PAIRS)
    own, *sends = call(split_kernel, pieces(128), [SMEM, VMEM, VMEM])(x_place, mine, got)
    got = three(sends, "grp", x_shift)
    got, top, bottom = lax.optimization_barrier((got, top, bottom))
    back, ahead = call(fold_kernel, [struct((ROWS, D), BF)] * 2, [VMEM] * 4)(g1, g3, top, bottom)
    own, *sends = call(split_kernel, pieces(32), [SMEM] + [VMEM] * 4)(y_place, own, *got)
    got = three(sends, "tile", y_shift)
    got, back, ahead = lax.optimization_barrier((got, back, ahead))
    value = call(add_kernel, struct((32, D), BF), [VMEM] * 4)(own, *got)
    home = [lax.ppermute(back, "tile", y_shift(-1)), lax.ppermute(ahead, "tile", y_shift(1))]
    got = [lax.ppermute(value, "tile", z_mirror(bits)) for bits in (1, 2, 3)]
    value = call(four_kernel, struct((32, D), BF), [VMEM] * 4)(value, *got)
    got = lax.ppermute(value, "tile", z_across())
    value = call(two_kernel, struct((32, D), BF), [VMEM] * 2)(value, got)
    value, home = lax.optimization_barrier((value, home))
    got = three([value] * 3, "tile", y_shift)
    value = call(join_kernel, struct((128, D), BF), [SMEM] + [VMEM] * 4)(y_place, value, *got)
    got = three([value] * 3, "grp", x_shift)
    value = call(join_kernel, struct((512, D), BF), [SMEM] + [VMEM] * 4)(x_place, value, *got)
    got = lax.ppermute(value, "grp", CORE_PAIRS)
    return call(final_kernel, struct((DIN, D), F32), [SMEM, VMEM, VMEM])(core, value, got), g0 + home[0] + home[1]


def shards(features, projection, pooled_grad, slide_counts, slide_offsets):
    group = lax.axis_index("grp")
    tile = lax.axis_index("tile")
    core, x_place = group % 2, group // 2
    y = tile % 4
    tiles = lax.axis_size("tile")
    info, outgoing = pl.pallas_call(
        plan_kernel,
        out_shape=[
            struct((SCALARS,), jnp.int32),
            struct((tiles,) + pooled_grad.shape[1:], BF),
        ],
        in_specs=[SMEM] * 3 + [VMEM],
        out_specs=[SMEM, VMEM],
        compiler_params=pltpu.CompilerParams(vmem_limit_bytes=16 << 20),
    )(jnp.stack([tile, core]).astype(jnp.int32), slide_counts, slide_offsets, pooled_grad)
    grads = lax.all_to_all(outgoing, "tile", 0, 0, tiled=True).reshape(D, D)

    half_rows = ROWS // 2

    def around_y(value):
        behind = lax.ppermute(value, "tile", y_shift(1))
        ahead = lax.ppermute(value, "tile", y_shift(-1))
        top = lax.ppermute(behind[:half_rows], "tile", y_shift(1))
        bottom = lax.ppermute(ahead[half_rows:], "tile", y_shift(-1))
        return value, behind, top, bottom, ahead

    pieces = around_y(features)
    mixed = [dot(piece, projection).astype(BF) for piece in pieces]
    message = struct((MESSAGE, 128), BF)
    first_part, last_part = call(
        sums_kernel,
        [message, message],
        [SMEM] + [VMEM] * 5,
        [pltpu.VMEM((PLANE, D), BF), pltpu.VMEM((6 * STRIP + 16, D), F32)],
        work=WORK,
    )(info, *mixed)
    local, local_row = call(
        local_kernel,
        [struct((D, D), F32), struct((8, D), F32)],
        [SMEM] + [VMEM] * 5,
        [pltpu.VMEM((PLANE, D), BF)],
        work=WORK,
    )(info, *mixed)
    flipped = call(flip_kernel, struct((DIN, PLANE), BF), [VMEM] * 5, work=WORK)(
        *pieces
    )

    around = [
        lax.ppermute(last_part, "tile", z_shift(1)),
        lax.ppermute(first_part, "tile", z_shift(-1)),
        lax.ppermute(last_part, "tile", z_shift(2)),
        lax.ppermute(first_part, "tile", z_shift(-2)),
    ]
    half = call(half_kernel, struct((D, D), F32), [VMEM])(grads)
    half, *around = lax.optimization_barrier((half, *around))
    extras = call(extras_kernel, [message] * 4, [SMEM] + [VMEM] * 4, work=WORK)(info, *around)
    extras = list(extras[:1]) + [
        lax.ppermute(extra, "tile", y_to_ends(step)) for step, extra in zip((1, 2, 3), extras[1:])
    ]

    wide = pltpu.VMEM((D, D), F32)
    narrow = pltpu.VMEM((D, D), BF)
    row_grads = call(
        pool_kernel,
        [struct((rows, D), BF) for _, _, rows in PIECES],
        [SMEM] + [VMEM] * 12,
        [pltpu.VMEM((len(PAIRS) * 128, 128), F32)] + [wide] * 3 + [pltpu.VMEM((D, 8), F32), pltpu.VMEM((8, D), F32)] + [narrow] * 6,
        26 << 20,
        WORK,
    )(info, local, local_row, *extras, half, *mixed)
    sent, mine = call(
        term_kernel,
        [struct((512, D), BF), struct((512, D), BF)],
        [SMEM] + [VMEM] * 6,
        [pltpu.VMEM((PLANE, D), BF)],
        work=WORK,
    )(info, *row_grads, flipped)

    projection_grad, row_grad = reduce_everywhere(sent, mine, row_grads, core, x_place, y)
    feature_grad = jnp.einsum(
        "rd,kd->rk", row_grad, projection, preferred_element_type=F32
    ).astype(BF)
    return (feature_grad, projection_grad)


def solution(mesh):
    placed = (P(("grp", "tile"), None), P(), P("grp", "tile", None), P("grp"), P("grp"))
    return jax.shard_map(
        shards,
        mesh=mesh,
        in_specs=placed,
        out_specs=(P(("grp", "tile"), None), P()),
        check_vma=False,
    )
```

```python
import functools

import jax
import jax.numpy as jnp
from jax import lax
from jax.experimental import pallas as pl
from jax.experimental.pallas import tpu as pltpu
from jax.sharding import PartitionSpec as P

BF = jnp.bfloat16
F32 = jnp.float32
ROWS = 256
PLANE = 4 * ROWS
DIN = 1024
D = 768
CHUNK = 256
CHUNKS = D // CHUNK
PAIRS = [(i, j) for i in range(6) for j in range(i + 1)]
STRIP = 32
TAIL = len(PAIRS) * STRIP
MESSAGE = TAIL + 16
PIECES = ((0, 0, ROWS), (1, 0, ROWS), (2, 0, ROWS // 2), (2, ROWS // 2, ROWS // 2), (3, 0, ROWS))
VMEM = pl.BlockSpec(memory_space=pltpu.VMEM)
SMEM = pl.BlockSpec(memory_space=pltpu.SMEM)

BASE, OWN, FIRST, LAST, QUARTER, GRAD, EXTRA, END, ALONE, PLACE = 0, 4, 6, 8, 10, 11, 12, 13, 14, 15
COUNT, SCALARS = 20, 21

WORK = 5 * 10**9
CORE_PAIRS = [(i, i ^ 1) for i in range(8)]


def x_shift(step):
    return [(x * 2 + c, (x + step) % 4 * 2 + c) for x in range(4) for c in range(2)]


def y_shift(step):
    return [(z * 4 + y, z * 4 + (y + step) % 4) for z in range(8) for y in range(4)]


def z_shift(step):
    return [(z * 4 + y, (z + step) % 8 * 4 + y) for z in range(8) for y in range(4)]


def y_to_ends(step):
    return [(z * 4 + (end - step) % 4, z * 4 + end) for z in range(8) for end in (0, 3)]


def z_across():
    pair = (6, 7, 4, 5, 2, 3, 0, 1)
    return [(z * 4 + y, pair[z] * 4 + y) for z in range(8) for y in range(4)]


def z_mirror(bits):
    return [(z * 4 + y, (z ^ bits) * 4 + y) for z in range(8) for y in range(4)]


def dot(a, b):
    return jnp.dot(a, b, preferred_element_type=F32)


def dot_rows(a, b):
    return lax.dot_general(a, b, (((0,), (0,)), ((), ())), preferred_element_type=F32)


def call(kernel, outs, specs, scratch=(), limit=16 << 20, work=None):
    cost = work and pl.CostEstimate(flops=work, bytes_accessed=10**7, transcendentals=0)
    return pl.pallas_call(
        kernel,
        out_shape=outs,
        in_specs=specs,
        out_specs=jax.tree.map(lambda _: VMEM, outs),
        scratch_shapes=list(scratch),
        cost_estimate=cost,
        compiler_params=pltpu.CompilerParams(vmem_limit_bytes=limit),
    )


def struct(shape, kind):
    return jax.ShapeDtypeStruct(shape, kind)


def plan_kernel(place, counts, offsets, grads, info, outgoing):
    total = offsets.shape[0]

    def slide_at(row):
        slide = jnp.int32(-1)
        for s in range(total):
            slide += (offsets[s] <= row).astype(jnp.int32)
        return slide

    def slide_for(at, first, last):
        inner = jnp.where(first + at < last, first + at, first)
        return jnp.where(at == 3, last, inner)

    def plan(plane, carry):
        first = slide_at(plane * PLANE)
        last = slide_at(plane * PLANE + PLANE - 1)
        for at in range(4):
            outgoing[plane * 4 + at] = grads[slide_for(at, first, last)]
        return carry

    lax.fori_loop(0, outgoing.shape[0] // 4, plan, 0)
    tile, core = place[0], place[1]
    y, z = lax.rem(tile, 4), lax.div(tile, 4)
    first, last = slide_at(z * PLANE), slide_at(z * PLANE + PLANE - 1)
    slide = slide_for(y, first, last)
    for start, index in ((OWN, slide), (FIRST, first), (LAST, last)):
        info[start] = offsets[index]
        info[start + 1] = offsets[index] + counts[index]
    for r in range(4):
        quarter = lax.rem(y + 4 - r, 4)
        info[BASE + r] = z * PLANE + quarter * ROWS
        info[PLACE + r] = quarter
    inside = (y == 0) | (y == 3) & (last > first) | (first + y < last) & (y < 3)
    after = offsets[jnp.minimum(last + 1, total - 1)]
    info[QUARTER] = y
    info[GRAD] = jnp.where(inside, info[OWN + 1], info[OWN])
    info[EXTRA] = ((y == 0) | (y == 3)).astype(jnp.int32)
    info[END] = jnp.where(last + 1 < total, after, outgoing.shape[0] * ROWS)
    info[ALONE] = (first == last).astype(jnp.int32)
    info[PLACE + 4] = core
    info[COUNT] = counts[slide]


def keep_rows(info, place, r, skip, rows, lanes):
    row = info[BASE + r] + skip + lax.broadcasted_iota(jnp.int32, (rows, lanes), 0)
    return (row >= info[place]) & (row < info[place + 1])


def store_kept(keep, x, out, start):
    rows = x.shape[0]
    for c in range(6):
        cols = slice(c * 128, (c + 1) * 128)
        out[start : start + rows, cols] = jnp.where(keep, x[:, cols], jnp.zeros((), BF))


def sums_kernel(info, x0, x1, top, bottom, x3, first_out, last_out, both, strips):
    line = lax.broadcasted_iota(jnp.int32, (1, PLANE), 1)
    place = jnp.zeros((1, PLANE), jnp.int32)
    for (r, skip, rows), x in zip(PIECES, (x0, x1, top, bottom, x3)):
        keep = keep_rows(info, FIRST, r, skip, rows, 128)
        keep = keep | keep_rows(info, LAST, r, skip, rows, 128)
        store_kept(keep, x, both, r * ROWS + skip)
        inside = (line >= r * ROWS + skip) & (line < r * ROWS + skip + rows)
        place = jnp.where(inside, line - r * ROWS + info[BASE + r], place)
    row = lax.broadcasted_iota(jnp.int32, (6 * STRIP, D), 0)
    col = lax.broadcasted_iota(jnp.int32, (6 * STRIP, D), 1)
    wanted = (row >> 5) * 128 + (row & (STRIP - 1)) + info[QUARTER] * STRIP
    select = jnp.where(col == wanted, 1.0, 0.0).astype(BF)
    chosen = lax.dot_general(
        select, both[...], (((1,), (1,)), ((), ())), preferred_element_type=F32
    )
    for start, out in ((FIRST, first_out), (LAST, last_out)):
        keep = (place >= info[start]) & (place < info[start + 1])
        kept = jnp.where(keep, chosen, 0.0).astype(BF)
        ones = jnp.broadcast_to(jnp.where(keep, 1.0, 0.0), (16, PLANE)).astype(BF)
        strips[...] = dot(jnp.concatenate([kept, ones], axis=0), both[...])
        for slot, (i, j) in enumerate(PAIRS):
            block = strips[i * STRIP : (i + 1) * STRIP, j * 128 : (j + 1) * 128]
            out[slot * STRIP : (slot + 1) * STRIP, :] = block.astype(BF)
        total = strips[6 * STRIP : 6 * STRIP + 8, :]
        high = total.astype(BF).astype(F32)
        low = total - high
        count = lax.broadcasted_iota(jnp.int32, (16, 128), 0)
        tail = jnp.zeros((16, 128), F32)
        for c in range(6):
            cut = slice(c * 128, (c + 1) * 128)
            tail = jnp.where(count == c, high[0:1, cut], tail)
            tail = jnp.where(count == 6 + c, low[0:1, cut], tail)
        out[TAIL:MESSAGE, :] = tail.astype(BF)


def local_kernel(info, x0, x1, top, bottom, x3, local, local_row, own):
    for (r, skip, rows), x in zip(PIECES, (x0, x1, top, bottom, x3)):
        store_kept(keep_rows(info, OWN, r, skip, rows, 128), x, own, r * ROWS + skip)
    for c in range(CHUNKS):
        here = pl.ds(c * CHUNK, CHUNK)
        local[here, :] = dot_rows(own[:, here], own[...])
    local_row[...] = dot(jnp.ones((8, PLANE), BF), own[...])


def flip_kernel(f0, f1, top, bottom, f3, out):
    start = 0
    for f in (f0, f1, top, bottom, f3):
        rows = f.shape[0]
        for c in range(DIN // CHUNK):
            here = pl.ds(c * CHUNK, CHUNK)
            out[here, start : start + rows] = f[:, here].astype(F32).T.astype(BF)
        start += rows


def fold_kernel(g1, g3, top, bottom, back, ahead):
    half = ROWS // 2
    back[0:half, :] = g1[0:half, :]
    back[half:ROWS, :] = g1[half:ROWS, :] + bottom[...]
    ahead[0:half, :] = g3[0:half, :] + top[...]
    ahead[half:ROWS, :] = g3[half:ROWS, :]


def extras_kernel(info, left_1, right_1, left_2, right_2, *outs):
    start = info[BASE] - info[QUARTER] * ROWS
    keeps = (
        info[FIRST] < start,
        info[END] > start + PLANE,
        info[FIRST] < start - PLANE,
        info[END] > start + 2 * PLANE,
    )
    values = [
        jnp.where(keep, value[...].astype(F32), 0.0)
        for keep, value in zip(keeps, (left_1, right_1, left_2, right_2))
    ]
    before = values[0] + values[2]
    after = values[1] + values[3]
    to_first = jnp.where(info[ALONE] > 0, before + after, before).astype(BF)
    to_last = after.astype(BF)
    for step, out in enumerate(outs):
        last = lax.rem(info[QUARTER] + step, 4) == 3

        @pl.when(last)
        def _():
            out[...] = to_last

        @pl.when(jnp.logical_not(last))
        def _():
            out[...] = to_first


def half_kernel(grads, out):
    for i in range(CHUNKS):
        for j in range(i, CHUNKS):
            rows = pl.ds(i * CHUNK, CHUNK)
            cols = pl.ds(j * CHUNK, CHUNK)
            upper = grads[rows, cols].astype(F32)
            lower = grads[cols, rows].astype(F32)
            block = 0.5 * (upper + lower.T)
            out[rows, cols] = block
            if i != j:
                out[cols, rows] = block.T


def total_of(value):
    return jnp.sum(value, axis=(0, 1), keepdims=True)


def pool_kernel(
    info, local, local_row, e0, e1, e2, e3, half, x0, x1, xt, xb, x3, g0, g1, gt, gb, g3,
    blocks, covar, wide_a, wide_b, mean_col, mean_row, scaled_b, first_b, top_b, second_b, under_b, grad_b,
):
    inverse = 1.0 / jnp.full((1, 1), info[COUNT], jnp.int32).astype(F32)
    covar[...] = local[...]
    mean_row[...] = local_row[...]

    @pl.when(info[EXTRA] > 0)
    def _():
        for r, extra in enumerate((e0, e1, e2, e3)):
            for slot in range(len(PAIRS)):
                row = pl.multiple_of(slot * 128 + info[PLACE + r] * STRIP, STRIP)
                piece = extra[slot * STRIP : (slot + 1) * STRIP, :]
                blocks[pl.ds(row, STRIP), :] = piece.astype(F32)
        for slot, (i, j) in enumerate(PAIRS):
            block = blocks[slot * 128 : (slot + 1) * 128, :]
            rows, cols = pl.ds(i * 128, 128), pl.ds(j * 128, 128)
            covar[rows, cols] += block
            if i != j:
                covar[cols, rows] += block.T

        tail = e0[TAIL:MESSAGE, :].astype(F32)
        for c in range(6):
            cut = pl.ds(c * 128, 128)
            mean_row[:, cut] += tail[c : c + 1, :] + tail[6 + c : 7 + c, :]

    mean_row[...] = mean_row[...] * inverse
    mean_col[...] = mean_row[...].T
    def each(body, start=0):
        def step(c, carry):
            return body(pl.ds(pl.multiple_of(c * CHUNK, CHUNK), CHUNK), carry)

        return lax.fori_loop(0, CHUNKS, step, start)

    def center(here, squares):
        value = covar[here, :] * inverse - mean_col[here, 0:1] * mean_row[0:1, :]
        covar[here, :] = value
        return squares + total_of(value * value)

    squares = each(center, jnp.zeros((1, 1), F32))
    norm = jnp.sqrt(squares + 1e-6)
    over = 1.0 / norm
    root = jnp.sqrt(norm)

    def scale_both(here, carry):
        scaled_b[here, :] = (covar[here, :] * over).astype(BF)
        top_b[here, :] = (half[here, :] * root).astype(BF)
        return carry

    each(scale_both)

    def make_first(here, carry):
        value = (1.5 * over) * covar[here, :] - 0.5 * dot(scaled_b[here, :], scaled_b[...])
        wide_a[here, :] = value
        first_b[here, :] = value.astype(BF)
        return carry

    each(make_first)

    def make_second(here, carry):
        value = 1.5 * wide_a[here, :] - 0.5 * dot(scaled_b[here, :], first_b[...])
        second_b[here, :] = value.astype(BF)
        under_b[here, :] = dot(first_b[here, :], top_b[...]).astype(BF)
        return carry

    each(make_second)

    def make_grad(here, sums):
        top = half[here, :] * root
        right = dot(top_b[here, :], second_b[...])
        sums += 1.5 * total_of(top * wide_a[here, :])
        sums -= 0.5 * total_of(right * first_b[here, :].astype(F32))
        value = 1.5 * top - 0.5 * (right + dot(second_b[here, :], top_b[...]))
        wide_b[here, :] = value
        grad_b[here, :] = value.astype(BF)
        return sums

    sums = each(make_grad, jnp.zeros((1, 1), F32))

    def make_scaled(here, inner):
        value = 1.5 * wide_b[here, :] + 0.25 * dot(under_b[here, :], first_b[...])
        value -= 0.5 * (dot(grad_b[here, :], scaled_b[...]) + dot(scaled_b[here, :], grad_b[...]))
        wide_a[here, :] = value
        return inner + total_of(value * covar[here, :])

    inner = each(make_scaled, jnp.zeros((1, 1), F32))
    grad_norm = sums * (0.5 * over) - inner * over * over
    scale = 2.0 * over * inverse

    def make_sym(here, mean_grad):
        value = (wide_a[here, :] + grad_norm * covar[here, :]) * scale
        second_b[here, :] = value.astype(BF)
        return mean_grad - jnp.sum(value * mean_col[here, 0:1], axis=0, keepdims=True)

    mean_grad = each(make_sym, jnp.zeros((1, D), F32))
    xs, gs = (x0, x1, xt, xb, x3), (g0, g1, gt, gb, g3)
    for (r, skip, rows), x, g in zip(PIECES, xs, gs):
        row = info[BASE + r] + skip + lax.broadcasted_iota(jnp.int32, (rows, D), 0)
        keep = (row >= info[OWN]) & (row < info[GRAD])
        value = dot(x[...], second_b[...]) + mean_grad
        g[...] = jnp.where(keep, value, 0.0).astype(BF)


def term_kernel(info, g0, g1, gt, gb, g3, flipped, sent, mine, plane):
    for (r, skip, rows), g in zip(PIECES, (g0, g1, gt, gb, g3)):
        plane[r * ROWS + skip : r * ROWS + skip + rows, :] = g[...]
    core = info[PLACE + 4]
    half = DIN // 2
    for place, out in ((1 - core, sent), (core, mine)):
        for c in range(half // CHUNK):
            here = pl.ds(pl.multiple_of(place * half + c * CHUNK, CHUNK), CHUNK)
            value = dot(flipped[here, :], plane[...])
            out[c * CHUNK : (c + 1) * CHUNK, :] = value.astype(out.dtype)


def split_kernel(place, mine, *refs):
    others, (own, *sends) = refs[: len(refs) - 4], refs[len(refs) - 4 :]
    rows = own.shape[0]

    def piece(step):
        here = pl.ds(pl.multiple_of(lax.rem(place[0] + step, 4) * rows, rows), rows)
        value = mine[here, :].astype(F32)
        for other in others:
            value = value + other[here, :].astype(F32)
        return value

    own[...] = piece(0)
    for step, out in zip((1, 3, 2), sends):
        out[...] = piece(step).astype(BF)


def add_kernel(mine, a, b, c, out):
    value = mine[...] + a[...].astype(F32) + b[...].astype(F32) + c[...].astype(F32)
    out[...] = value.astype(BF)


def four_kernel(own, a, b, c, out):
    near = own[...].astype(F32) + a[...].astype(F32)
    out[...] = (near + (b[...].astype(F32) + c[...].astype(F32))).astype(BF)


def two_kernel(own, other, out):
    out[...] = (own[...].astype(F32) + other[...].astype(F32)).astype(BF)


def join_kernel(place, own, a, b, c, out):
    rows = own.shape[0]
    for step, value in ((0, own), (1, a), (3, b), (2, c)):
        index = lax.rem(place[0] + 4 - step, 4)
        out[pl.ds(pl.multiple_of(index * rows, rows), rows), :] = value[...]


def final_kernel(core, own, other, out):
    rows = own.shape[0]
    out[pl.ds(pl.multiple_of(core[0] * rows, rows), rows), :] = own[...].astype(F32)
    out[pl.ds(pl.multiple_of((1 - core[0]) * rows, rows), rows), :] = other[...].astype(F32)


def three(values, axis, shift):
    return [lax.ppermute(v, axis, shift(step)) for step, v in zip((1, 3, 2), values)]


def reduce_everywhere(sent, mine, row_grads, core, x_place, y_place):
    g0, g1, top, bottom, g3 = row_grads
    top = lax.ppermute(top, "tile", y_shift(1))
    bottom = lax.ppermute(bottom, "tile", y_shift(-1))
    core, x_place, y_place = core[None], x_place[None], y_place[None]

    def pieces(rows):
        return [struct((rows, D), F32)] + [struct((rows, D), BF)] * 3

    got = lax.ppermute(sent, "grp", CORE_PAIRS)
    own, *sends = call(split_kernel, pieces(128), [SMEM, VMEM, VMEM])(x_place, mine, got)
    got = three(sends, "grp", x_shift)
    got, top, bottom = lax.optimization_barrier((got, top, bottom))
    back, ahead = call(fold_kernel, [struct((ROWS, D), BF)] * 2, [VMEM] * 4)(g1, g3, top, bottom)
    own, *sends = call(split_kernel, pieces(32), [SMEM] + [VMEM] * 4)(y_place, own, *got)
    got = three(sends, "tile", y_shift)
    got, back, ahead = lax.optimization_barrier((got, back, ahead))
    value = call(add_kernel, struct((32, D), BF), [VMEM] * 4)(own, *got)
    home = [lax.ppermute(back, "tile", y_shift(-1)), lax.ppermute(ahead, "tile", y_shift(1))]
    got = [lax.ppermute(value, "tile", z_mirror(bits)) for bits in (1, 2, 3)]
    value = call(four_kernel, struct((32, D), BF), [VMEM] * 4)(value, *got)
    got = lax.ppermute(value, "tile", z_across())
    value = call(two_kernel, struct((32, D), BF), [VMEM] * 2)(value, got)
    value, home = lax.optimization_barrier((value, home))
    got = three([value] * 3, "tile", y_shift)
    value = call(join_kernel, struct((128, D), BF), [SMEM] + [VMEM] * 4)(y_place, value, *got)
    got = three([value] * 3, "grp", x_shift)
    value = call(join_kernel, struct((512, D), BF), [SMEM] + [VMEM] * 4)(x_place, value, *got)
    got = lax.ppermute(value, "grp", CORE_PAIRS)
    return call(final_kernel, struct((DIN, D), F32), [SMEM, VMEM, VMEM])(core, value, got), g0 + home[0] + home[1]


def shards(features, projection, pooled_grad, slide_counts, slide_offsets):
    group = lax.axis_index("grp")
    tile = lax.axis_index("tile")
    core, x_place = group % 2, group // 2
    y = tile % 4
    tiles = lax.axis_size("tile")
    info, outgoing = pl.pallas_call(
        plan_kernel,
        out_shape=[
            struct((SCALARS,), jnp.int32),
            struct((tiles,) + pooled_grad.shape[1:], BF),
        ],
        in_specs=[SMEM] * 3 + [VMEM],
        out_specs=[SMEM, VMEM],
        compiler_params=pltpu.CompilerParams(vmem_limit_bytes=16 << 20),
    )(jnp.stack([tile, core]).astype(jnp.int32), slide_counts, slide_offsets, pooled_grad)
    grads = lax.all_to_all(outgoing, "tile", 0, 0, tiled=True).reshape(D, D)

    half_rows = ROWS // 2

    def around_y(value):
        behind = lax.ppermute(value, "tile", y_shift(1))
        ahead = lax.ppermute(value, "tile", y_shift(-1))
        top = lax.ppermute(behind[:half_rows], "tile", y_shift(1))
        bottom = lax.ppermute(ahead[half_rows:], "tile", y_shift(-1))
        return value, behind, top, bottom, ahead

    pieces = around_y(features)
    mixed = [dot(piece, projection).astype(BF) for piece in pieces]
    message = struct((MESSAGE, 128), BF)
    first_part, last_part = call(
        sums_kernel,
        [message, message],
        [SMEM] + [VMEM] * 5,
        [pltpu.VMEM((PLANE, D), BF), pltpu.VMEM((6 * STRIP + 16, D), F32)],
        work=WORK,
    )(info, *mixed)
    local, local_row = call(
        local_kernel,
        [struct((D, D), F32), struct((8, D), F32)],
        [SMEM] + [VMEM] * 5,
        [pltpu.VMEM((PLANE, D), BF)],
        work=WORK,
    )(info, *mixed)
    flipped = call(flip_kernel, struct((DIN, PLANE), BF), [VMEM] * 5, work=WORK)(
        *pieces
    )

    around = [
        lax.ppermute(last_part, "tile", z_shift(1)),
        lax.ppermute(first_part, "tile", z_shift(-1)),
        lax.ppermute(last_part, "tile", z_shift(2)),
        lax.ppermute(first_part, "tile", z_shift(-2)),
    ]
    half = call(half_kernel, struct((D, D), F32), [VMEM])(grads)
    half, *around = lax.optimization_barrier((half, *around))
    extras = call(extras_kernel, [message] * 4, [SMEM] + [VMEM] * 4, work=WORK)(info, *around)
    extras = list(extras[:1]) + [
        lax.ppermute(extra, "tile", y_to_ends(step)) for step, extra in zip((1, 2, 3), extras[1:])
    ]

    wide = pltpu.VMEM((D, D), F32)
    narrow = pltpu.VMEM((D, D), BF)
    row_grads = call(
        pool_kernel,
        [struct((rows, D), BF) for _, _, rows in PIECES],
        [SMEM] + [VMEM] * 12,
        [pltpu.VMEM((len(PAIRS) * 128, 128), F32)] + [wide] * 3 + [pltpu.VMEM((D, 8), F32), pltpu.VMEM((8, D), F32)] + [narrow] * 6,
        26 << 20,
        WORK,
    )(info, local, local_row, *extras, half, *mixed)
    sent, mine = call(
        term_kernel,
        [struct((512, D), BF), struct((512, D), BF)],
        [SMEM] + [VMEM] * 6,
        [pltpu.VMEM((PLANE, D), BF)],
        work=WORK,
    )(info, *row_grads, flipped)

    projection_grad, row_grad = reduce_everywhere(sent, mine, row_grads, core, x_place, y)
    feature_grad = jnp.einsum(
        "rd,kd->rk", row_grad, projection, preferred_element_type=F32
    ).astype(BF)
    return (feature_grad, projection_grad)


def solution(mesh):
    placed = (P(("grp", "tile"), None), P(), P("grp", "tile", None), P("grp"), P("grp"))
    return jax.shard_map(
        shards,
        mesh=mesh,
        in_specs=placed,
        out_specs=(P(("grp", "tile"), None), P()),
        check_vma=False,
    )
```

```python
import functools

import jax
import jax.numpy as jnp
from jax import lax
from jax.experimental import pallas as pl
from jax.experimental.pallas import tpu as pltpu
from jax.sharding import PartitionSpec as P

BF = jnp.bfloat16
F32 = jnp.float32
ROWS = 256
PLANE = 4 * ROWS
DIN = 1024
D = 768
CHUNK = 256
CHUNKS = D // CHUNK
PAIRS = [(i, j) for i in range(6) for j in range(i + 1)]
STRIP = 32
TAIL = len(PAIRS) * STRIP
MESSAGE = TAIL + 16
PIECES = ((0, 0, ROWS), (1, 0, ROWS), (2, 0, ROWS // 2), (2, ROWS // 2, ROWS // 2), (3, 0, ROWS))
VMEM = pl.BlockSpec(memory_space=pltpu.VMEM)
SMEM = pl.BlockSpec(memory_space=pltpu.SMEM)

BASE, OWN, FIRST, LAST, QUARTER, GRAD, EXTRA, END, ALONE, PLACE = 0, 4, 6, 8, 10, 11, 12, 13, 14, 15
COUNT, SCALARS = 20, 21

WORK = 5 * 10**9
CORE_PAIRS = [(i, i ^ 1) for i in range(8)]


def x_shift(step):
    return [(x * 2 + c, (x + step) % 4 * 2 + c) for x in range(4) for c in range(2)]


def y_shift(step):
    return [(z * 4 + y, z * 4 + (y + step) % 4) for z in range(8) for y in range(4)]


def z_shift(step):
    return [(z * 4 + y, (z + step) % 8 * 4 + y) for z in range(8) for y in range(4)]


def y_to_ends(step):
    return [(z * 4 + (end - step) % 4, z * 4 + end) for z in range(8) for end in (0, 3)]


def z_across():
    pair = (6, 7, 4, 5, 2, 3, 0, 1)
    return [(z * 4 + y, pair[z] * 4 + y) for z in range(8) for y in range(4)]


def z_mirror(bits):
    return [(z * 4 + y, (z ^ bits) * 4 + y) for z in range(8) for y in range(4)]


def dot(a, b):
    return jnp.dot(a, b, preferred_element_type=F32)


def dot_rows(a, b):
    return lax.dot_general(a, b, (((0,), (0,)), ((), ())), preferred_element_type=F32)


def call(kernel, outs, specs, scratch=(), limit=16 << 20, work=None):
    cost = work and pl.CostEstimate(flops=work, bytes_accessed=10**7, transcendentals=0)
    return pl.pallas_call(
        kernel,
        out_shape=outs,
        in_specs=specs,
        out_specs=jax.tree.map(lambda _: VMEM, outs),
        scratch_shapes=list(scratch),
        cost_estimate=cost,
        compiler_params=pltpu.CompilerParams(vmem_limit_bytes=limit),
    )


def struct(shape, kind):
    return jax.ShapeDtypeStruct(shape, kind)


def plan_kernel(place, counts, offsets, grads, info, outgoing):
    total = offsets.shape[0]

    def slide_at(row):
        slide = jnp.int32(-1)
        for s in range(total):
            slide += (offsets[s] <= row).astype(jnp.int32)
        return slide

    def slide_for(at, first, last):
        inner = jnp.where(first + at < last, first + at, first)
        return jnp.where(at == 3, last, inner)

    def plan(plane, carry):
        first = slide_at(plane * PLANE)
        last = slide_at(plane * PLANE + PLANE - 1)
        for at in range(4):
            outgoing[plane * 4 + at] = grads[slide_for(at, first, last)]
        return carry

    lax.fori_loop(0, outgoing.shape[0] // 4, plan, 0)
    tile, core = place[0], place[1]
    y, z = lax.rem(tile, 4), lax.div(tile, 4)
    first, last = slide_at(z * PLANE), slide_at(z * PLANE + PLANE - 1)
    slide = slide_for(y, first, last)
    for start, index in ((OWN, slide), (FIRST, first), (LAST, last)):
        info[start] = offsets[index]
        info[start + 1] = offsets[index] + counts[index]
    for r in range(4):
        quarter = lax.rem(y + 4 - r, 4)
        info[BASE + r] = z * PLANE + quarter * ROWS
        info[PLACE + r] = quarter
    inside = (y == 0) | (y == 3) & (last > first) | (first + y < last) & (y < 3)
    after = offsets[jnp.minimum(last + 1, total - 1)]
    info[QUARTER] = y
    info[GRAD] = jnp.where(inside, info[OWN + 1], info[OWN])
    info[EXTRA] = ((y == 0) | (y == 3)).astype(jnp.int32)
    info[END] = jnp.where(last + 1 < total, after, outgoing.shape[0] * ROWS)
    info[ALONE] = (first == last).astype(jnp.int32)
    info[PLACE + 4] = core
    info[COUNT] = counts[slide]


def keep_rows(info, place, r, skip, rows, lanes):
    row = info[BASE + r] + skip + lax.broadcasted_iota(jnp.int32, (rows, lanes), 0)
    return (row >= info[place]) & (row < info[place + 1])


def store_kept(keep, x, out, start):
    rows = x.shape[0]
    for c in range(6):
        cols = slice(c * 128, (c + 1) * 128)
        out[start : start + rows, cols] = jnp.where(keep, x[:, cols], jnp.zeros((), BF))


def sums_kernel(info, x0, x1, top, bottom, x3, first_out, last_out, both, strips):
    line = lax.broadcasted_iota(jnp.int32, (1, PLANE), 1)
    place = jnp.zeros((1, PLANE), jnp.int32)
    for (r, skip, rows), x in zip(PIECES, (x0, x1, top, bottom, x3)):
        keep = keep_rows(info, FIRST, r, skip, rows, 128)
        keep = keep | keep_rows(info, LAST, r, skip, rows, 128)
        store_kept(keep, x, both, r * ROWS + skip)
        inside = (line >= r * ROWS + skip) & (line < r * ROWS + skip + rows)
        place = jnp.where(inside, line - r * ROWS + info[BASE + r], place)
    row = lax.broadcasted_iota(jnp.int32, (6 * STRIP, D), 0)
    col = lax.broadcasted_iota(jnp.int32, (6 * STRIP, D), 1)
    wanted = (row >> 5) * 128 + (row & (STRIP - 1)) + info[QUARTER] * STRIP
    select = jnp.where(col == wanted, 1.0, 0.0).astype(BF)
    chosen = lax.dot_general(
        select, both[...], (((1,), (1,)), ((), ())), preferred_element_type=F32
    )
    for start, out in ((FIRST, first_out), (LAST, last_out)):
        keep = (place >= info[start]) & (place < info[start + 1])
        kept = jnp.where(keep, chosen, 0.0).astype(BF)
        ones = jnp.broadcast_to(jnp.where(keep, 1.0, 0.0), (16, PLANE)).astype(BF)
        strips[...] = dot(jnp.concatenate([kept, ones], axis=0), both[...])
        for slot, (i, j) in enumerate(PAIRS):
            block = strips[i * STRIP : (i + 1) * STRIP, j * 128 : (j + 1) * 128]
            out[slot * STRIP : (slot + 1) * STRIP, :] = block.astype(BF)
        total = strips[6 * STRIP : 6 * STRIP + 8, :]
        high = total.astype(BF).astype(F32)
        low = total - high
        count = lax.broadcasted_iota(jnp.int32, (16, 128), 0)
        tail = jnp.zeros((16, 128), F32)
        for c in range(6):
            cut = slice(c * 128, (c + 1) * 128)
            tail = jnp.where(count == c, high[0:1, cut], tail)
            tail = jnp.where(count == 6 + c, low[0:1, cut], tail)
        out[TAIL:MESSAGE, :] = tail.astype(BF)


def local_kernel(info, x0, x1, top, bottom, x3, local, local_row, own):
    for (r, skip, rows), x in zip(PIECES, (x0, x1, top, bottom, x3)):
        store_kept(keep_rows(info, OWN, r, skip, rows, 128), x, own, r * ROWS + skip)

    def step(c, carry):
        here = pl.ds(pl.multiple_of(c * CHUNK, CHUNK), CHUNK)
        local[here, :] = dot_rows(own[:, here], own[...])
        return carry

    lax.fori_loop(0, CHUNKS, step, 0)
    local_row[...] = dot(jnp.ones((8, PLANE), BF), own[...])


def flip_kernel(f0, f1, top, bottom, f3, out):
    start = 0
    for f in (f0, f1, top, bottom, f3):
        rows = f.shape[0]

        def step(c, carry, f=f, start=start, rows=rows):
            here = pl.ds(pl.multiple_of(c * CHUNK, CHUNK), CHUNK)
            out[here, start : start + rows] = f[:, here].astype(F32).T.astype(BF)
            return carry

        lax.fori_loop(0, DIN // CHUNK, step, 0)
        start += rows


def fold_kernel(g1, g3, top, bottom, back, ahead):
    half = ROWS // 2
    back[0:half, :] = g1[0:half, :]
    back[half:ROWS, :] = g1[half:ROWS, :] + bottom[...]
    ahead[0:half, :] = g3[0:half, :] + top[...]
    ahead[half:ROWS, :] = g3[half:ROWS, :]


def extras_kernel(info, left_1, right_1, left_2, right_2, *outs):
    start = info[BASE] - info[QUARTER] * ROWS
    keeps = (
        info[FIRST] < start,
        info[END] > start + PLANE,
        info[FIRST] < start - PLANE,
        info[END] > start + 2 * PLANE,
    )
    values = [
        jnp.where(keep, value[...].astype(F32), 0.0)
        for keep, value in zip(keeps, (left_1, right_1, left_2, right_2))
    ]
    before = values[0] + values[2]
    after = values[1] + values[3]
    to_first = jnp.where(info[ALONE] > 0, before + after, before).astype(BF)
    to_last = after.astype(BF)
    for step, out in enumerate(outs):
        last = lax.rem(info[QUARTER] + step, 4) == 3

        @pl.when(last)
        def _():
            out[...] = to_last

        @pl.when(jnp.logical_not(last))
        def _():
            out[...] = to_first


def half_kernel(grads, out):
    for i in range(CHUNKS):
        for j in range(i, CHUNKS):
            rows = pl.ds(i * CHUNK, CHUNK)
            cols = pl.ds(j * CHUNK, CHUNK)
            upper = grads[rows, cols].astype(F32)
            lower = grads[cols, rows].astype(F32)
            block = 0.5 * (upper + lower.T)
            out[rows, cols] = block
            if i != j:
                out[cols, rows] = block.T


def total_of(value):
    return jnp.sum(value, axis=(0, 1), keepdims=True)


def pool_kernel(
    info, local, local_row, e0, e1, e2, e3, half, x0, x1, xt, xb, x3, g0, g1, gt, gb, g3,
    blocks, covar, wide_a, wide_b, mean_col, mean_row, scaled_b, first_b, top_b, second_b, under_b, grad_b,
):
    inverse = 1.0 / jnp.full((1, 1), info[COUNT], jnp.int32).astype(F32)
    covar[...] = local[...]
    mean_row[...] = local_row[...]

    @pl.when(info[EXTRA] > 0)
    def _():
        for r, extra in enumerate((e0, e1, e2, e3)):
            for slot in range(len(PAIRS)):
                row = pl.multiple_of(slot * 128 + info[PLACE + r] * STRIP, STRIP)
                piece = extra[slot * STRIP : (slot + 1) * STRIP, :]
                blocks[pl.ds(row, STRIP), :] = piece.astype(F32)
        for slot, (i, j) in enumerate(PAIRS):
            block = blocks[slot * 128 : (slot + 1) * 128, :]
            rows, cols = pl.ds(i * 128, 128), pl.ds(j * 128, 128)
            covar[rows, cols] += block
            if i != j:
                covar[cols, rows] += block.T

        tail = e0[TAIL:MESSAGE, :].astype(F32)
        for c in range(6):
            cut = pl.ds(c * 128, 128)
            mean_row[:, cut] += tail[c : c + 1, :] + tail[6 + c : 7 + c, :]

    mean_row[...] = mean_row[...] * inverse
    mean_col[...] = mean_row[...].T
    def each(body, start=0):
        def step(c, carry):
            return body(pl.ds(pl.multiple_of(c * 384, 384), 384), carry)

        return lax.fori_loop(0, D // 384, step, start)

    def center(here, squares):
        value = covar[here, :] * inverse - mean_col[here, 0:1] * mean_row[0:1, :]
        covar[here, :] = value
        return squares + total_of(value * value)

    squares = each(center, jnp.zeros((1, 1), F32))
    norm = jnp.sqrt(squares + 1e-6)
    over = 1.0 / norm
    root = jnp.sqrt(norm)

    def scale_both(here, carry):
        scaled_b[here, :] = (covar[here, :] * over).astype(BF)
        top_b[here, :] = (half[here, :] * root).astype(BF)
        return carry

    each(scale_both)

    def make_first(here, carry):
        value = (1.5 * over) * covar[here, :] - 0.5 * dot(scaled_b[here, :], scaled_b[...])
        wide_a[here, :] = value
        first_b[here, :] = value.astype(BF)
        return carry

    each(make_first)

    def make_second(here, carry):
        value = 1.5 * wide_a[here, :] - 0.5 * dot(scaled_b[here, :], first_b[...])
        second_b[here, :] = value.astype(BF)
        under_b[here, :] = dot(first_b[here, :], top_b[...]).astype(BF)
        return carry

    each(make_second)

    def make_grad(here, sums):
        top = half[here, :] * root
        right = dot(top_b[here, :], second_b[...])
        sums += 1.5 * total_of(top * wide_a[here, :])
        sums -= 0.5 * total_of(right * first_b[here, :].astype(F32))
        value = 1.5 * top - 0.5 * (right + dot(second_b[here, :], top_b[...]))
        wide_b[here, :] = value
        grad_b[here, :] = value.astype(BF)
        return sums

    sums = each(make_grad, jnp.zeros((1, 1), F32))

    def make_scaled(here, inner):
        value = 1.5 * wide_b[here, :] + 0.25 * dot(under_b[here, :], first_b[...])
        value -= 0.5 * (dot(grad_b[here, :], scaled_b[...]) + dot(scaled_b[here, :], grad_b[...]))
        wide_a[here, :] = value
        return inner + total_of(value * covar[here, :])

    inner = each(make_scaled, jnp.zeros((1, 1), F32))
    grad_norm = sums * (0.5 * over) - inner * over * over
    scale = 2.0 * over * inverse

    def make_sym(here, mean_grad):
        value = (wide_a[here, :] + grad_norm * covar[here, :]) * scale
        second_b[here, :] = value.astype(BF)
        return mean_grad - jnp.sum(value * mean_col[here, 0:1], axis=0, keepdims=True)

    mean_grad = each(make_sym, jnp.zeros((1, D), F32))
    xs, gs = (x0, x1, xt, xb, x3), (g0, g1, gt, gb, g3)
    for (r, skip, rows), x, g in zip(PIECES, xs, gs):
        row = info[BASE + r] + skip + lax.broadcasted_iota(jnp.int32, (rows, D), 0)
        keep = (row >= info[OWN]) & (row < info[GRAD])
        value = dot(x[...], second_b[...]) + mean_grad
        g[...] = jnp.where(keep, value, 0.0).astype(BF)


def term_kernel(info, g0, g1, gt, gb, g3, flipped, sent, mine, plane):
    for (r, skip, rows), g in zip(PIECES, (g0, g1, gt, gb, g3)):
        plane[r * ROWS + skip : r * ROWS + skip + rows, :] = g[...]
    core = info[PLACE + 4]
    half = DIN // 2
    for place, out in ((1 - core, sent), (core, mine)):

        def step(c, carry, place=place, out=out):
            here = pl.ds(pl.multiple_of(place * half + c * CHUNK, CHUNK), CHUNK)
            value = dot(flipped[here, :], plane[...])
            out[pl.ds(pl.multiple_of(c * CHUNK, CHUNK), CHUNK), :] = value.astype(out.dtype)
            return carry

        lax.fori_loop(0, half // CHUNK, step, 0)


def split_kernel(place, mine, *refs):
    others, (own, *sends) = refs[: len(refs) - 4], refs[len(refs) - 4 :]
    rows = own.shape[0]

    def piece(step):
        here = pl.ds(pl.multiple_of(lax.rem(place[0] + step, 4) * rows, rows), rows)
        value = mine[here, :].astype(F32)
        for other in others:
            value = value + other[here, :].astype(F32)
        return value

    own[...] = piece(0)
    for step, out in zip((1, 3, 2), sends):
        out[...] = piece(step).astype(BF)


def add_kernel(mine, a, b, c, out):
    value = mine[...] + a[...].astype(F32) + b[...].astype(F32) + c[...].astype(F32)
    out[...] = value.astype(BF)


def four_kernel(own, a, b, c, out):
    near = own[...].astype(F32) + a[...].astype(F32)
    out[...] = (near + (b[...].astype(F32) + c[...].astype(F32))).astype(BF)


def two_kernel(own, other, out):
    out[...] = (own[...].astype(F32) + other[...].astype(F32)).astype(BF)


def join_kernel(place, own, a, b, c, out):
    rows = own.shape[0]
    for step, value in ((0, own), (1, a), (3, b), (2, c)):
        index = lax.rem(place[0] + 4 - step, 4)
        out[pl.ds(pl.multiple_of(index * rows, rows), rows), :] = value[...]


def final_kernel(core, own, other, out):
    rows = own.shape[0]

    def step(c, carry):
        here = pl.ds(pl.multiple_of(c * 128, 128), 128)
        for place, value in ((core[0], own), (1 - core[0], other)):
            out[pl.ds(pl.multiple_of(place * rows + c * 128, 128), 128), :] = value[here, :].astype(F32)
        return carry

    lax.fori_loop(0, rows // 128, step, 0)


def three(values, axis, shift):
    return [lax.ppermute(v, axis, shift(step)) for step, v in zip((1, 3, 2), values)]


def reduce_everywhere(sent, mine, row_grads, core, x_place, y_place):
    g0, g1, top, bottom, g3 = row_grads
    top = lax.ppermute(top, "tile", y_shift(1))
    bottom = lax.ppermute(bottom, "tile", y_shift(-1))
    core, x_place, y_place = core[None], x_place[None], y_place[None]

    def pieces(rows):
        return [struct((rows, D), F32)] + [struct((rows, D), BF)] * 3

    got = lax.ppermute(sent, "grp", CORE_PAIRS)
    own, *sends = call(split_kernel, pieces(128), [SMEM, VMEM, VMEM])(x_place, mine, got)
    got = three(sends, "grp", x_shift)
    got, top, bottom = lax.optimization_barrier((got, top, bottom))
    back, ahead = call(fold_kernel, [struct((ROWS, D), BF)] * 2, [VMEM] * 4)(g1, g3, top, bottom)
    own, *sends = call(split_kernel, pieces(32), [SMEM] + [VMEM] * 4)(y_place, own, *got)
    got = three(sends, "tile", y_shift)
    got, back, ahead = lax.optimization_barrier((got, back, ahead))
    value = call(add_kernel, struct((32, D), BF), [VMEM] * 4)(own, *got)
    home = [lax.ppermute(back, "tile", y_shift(-1)), lax.ppermute(ahead, "tile", y_shift(1))]
    got = [lax.ppermute(value, "tile", z_mirror(bits)) for bits in (1, 2, 3)]
    value = call(four_kernel, struct((32, D), BF), [VMEM] * 4)(value, *got)
    got = lax.ppermute(value, "tile", z_across())
    value = call(two_kernel, struct((32, D), BF), [VMEM] * 2)(value, got)
    value, home = lax.optimization_barrier((value, home))
    got = three([value] * 3, "tile", y_shift)
    value = call(join_kernel, struct((128, D), BF), [SMEM] + [VMEM] * 4)(y_place, value, *got)
    got = three([value] * 3, "grp", x_shift)
    value = call(join_kernel, struct((512, D), BF), [SMEM] + [VMEM] * 4)(x_place, value, *got)
    got = lax.ppermute(value, "grp", CORE_PAIRS)
    return call(final_kernel, struct((DIN, D), F32), [SMEM, VMEM, VMEM])(core, value, got), g0 + home[0] + home[1]


def shards(features, projection, pooled_grad, slide_counts, slide_offsets):
    group = lax.axis_index("grp")
    tile = lax.axis_index("tile")
    core, x_place = group % 2, group // 2
    y = tile % 4
    tiles = lax.axis_size("tile")
    info, outgoing = pl.pallas_call(
        plan_kernel,
        out_shape=[
            struct((SCALARS,), jnp.int32),
            struct((tiles,) + pooled_grad.shape[1:], BF),
        ],
        in_specs=[SMEM] * 3 + [VMEM],
        out_specs=[SMEM, VMEM],
        compiler_params=pltpu.CompilerParams(vmem_limit_bytes=16 << 20),
    )(jnp.stack([tile, core]).astype(jnp.int32), slide_counts, slide_offsets, pooled_grad)
    grads = lax.all_to_all(outgoing, "tile", 0, 0, tiled=True).reshape(D, D)

    half_rows = ROWS // 2

    def around_y(value):
        behind = lax.ppermute(value, "tile", y_shift(1))
        ahead = lax.ppermute(value, "tile", y_shift(-1))
        top = lax.ppermute(behind[:half_rows], "tile", y_shift(1))
        bottom = lax.ppermute(ahead[half_rows:], "tile", y_shift(-1))
        return value, behind, top, bottom, ahead

    pieces = around_y(features)
    mixed = [dot(piece, projection).astype(BF) for piece in pieces]
    message = struct((MESSAGE, 128), BF)
    first_part, last_part = call(
        sums_kernel,
        [message, message],
        [SMEM] + [VMEM] * 5,
        [pltpu.VMEM((PLANE, D), BF), pltpu.VMEM((6 * STRIP + 16, D), F32)],
        work=WORK,
    )(info, *mixed)
    local, local_row = call(
        local_kernel,
        [struct((D, D), F32), struct((8, D), F32)],
        [SMEM] + [VMEM] * 5,
        [pltpu.VMEM((PLANE, D), BF)],
        work=WORK,
    )(info, *mixed)
    flipped = call(flip_kernel, struct((DIN, PLANE), BF), [VMEM] * 5, work=WORK)(
        *pieces
    )

    around = [
        lax.ppermute(last_part, "tile", z_shift(1)),
        lax.ppermute(first_part, "tile", z_shift(-1)),
        lax.ppermute(last_part, "tile", z_shift(2)),
        lax.ppermute(first_part, "tile", z_shift(-2)),
    ]
    half = call(half_kernel, struct((D, D), F32), [VMEM])(grads)
    half, *around = lax.optimization_barrier((half, *around))
    extras = call(extras_kernel, [message] * 4, [SMEM] + [VMEM] * 4, work=WORK)(info, *around)
    extras = list(extras[:1]) + [
        lax.ppermute(extra, "tile", y_to_ends(step)) for step, extra in zip((1, 2, 3), extras[1:])
    ]

    wide = pltpu.VMEM((D, D), F32)
    narrow = pltpu.VMEM((D, D), BF)
    row_grads = call(
        pool_kernel,
        [struct((rows, D), BF) for _, _, rows in PIECES],
        [SMEM] + [VMEM] * 12,
        [pltpu.VMEM((len(PAIRS) * 128, 128), F32)] + [wide] * 3 + [pltpu.VMEM((D, 8), F32), pltpu.VMEM((8, D), F32)] + [narrow] * 6,
        26 << 20,
        WORK,
    )(info, local, local_row, *extras, half, *mixed)
    sent, mine = call(
        term_kernel,
        [struct((512, D), BF), struct((512, D), BF)],
        [SMEM] + [VMEM] * 6,
        [pltpu.VMEM((PLANE, D), BF)],
        work=WORK,
    )(info, *row_grads, flipped)

    projection_grad, row_grad = reduce_everywhere(sent, mine, row_grads, core, x_place, y)
    feature_grad = jnp.einsum(
        "rd,kd->rk", row_grad, projection, preferred_element_type=F32
    ).astype(BF)
    return (feature_grad, projection_grad)


def solution(mesh):
    placed = (P(("grp", "tile"), None), P(), P("grp", "tile", None), P("grp"), P("grp"))
    return jax.shard_map(
        shards,
        mesh=mesh,
        in_specs=placed,
        out_specs=(P(("grp", "tile"), None), P()),
        check_vma=False,
    )
```
